32 devices in a mesh: dp: 16 (over z, y, core), tensor: 2 (over x).
Axes of the slice: x: 2, y: 2, z: 4, core: 2. Of those that a mesh axis runs over, the one named last changes fastest.
Arguments:
- tokens: bfloat16 [6, 1024, 2048], P(None, 'dp'), may hold values from -6 to 6
- cotangent: bfloat16 [6, 1024, 2048], P(None, 'dp'), may hold values from -6 to 6
- active: int32 [3, 2], replicated, may hold values from 0 to 1, as said below
- assignment: int32 [6], replicated, may hold values from 0 to 5, each once
- attention_gain: bfloat16 [2048], P('dp'), may hold values from 0.099609375 to 1.8984375
- query_weight: bfloat16 [2048, 2048], P('dp', 'tensor'), may hold values from -0.1875 to 0.1875
- key_weight: bfloat16 [2048, 512], P('dp', 'tensor'), may hold values from -0.125 to 0.125
- value_weight: bfloat16 [2048, 512], P('dp', 'tensor'), may hold values from -0.125 to 0.125
- out_weight: bfloat16 [2048, 2048], P('tensor', 'dp'), may hold values from -2 to 2
- feedforward_gain: bfloat16 [2048], P('dp'), may hold values from 0.099609375 to 1.8984375
- gate_weight: bfloat16 [2048, 5632], P('dp', 'tensor'), may hold values from -0.125 to 0.125
- up_weight: bfloat16 [2048, 5632], P('dp', 'tensor'), may hold values from -0.125 to 0.125
- down_weight: bfloat16 [5632, 2048], P('tensor', 'dp'), may hold values from -0.109375 to 0.109375
Outputs:
- result: bfloat16 [6, 1024, 2048], P(None, 'dp')
- input_grad: float32 [6, 1024, 2048], P(None, 'dp')
- attention_gain_grad: float32 [2048], P('dp')
- query_weight_grad: float32 [2048, 2048], P('dp', 'tensor')
- key_weight_grad: float32 [2048, 512], P('dp', 'tensor')
- value_weight_grad: float32 [2048, 512], P('dp', 'tensor')
- out_weight_grad: float32 [2048, 2048], P('tensor', 'dp')
- feedforward_gain_grad: float32 [2048], P('dp')
- gate_weight_grad: float32 [2048, 5632], P('dp', 'tensor')
- up_weight_grad: float32 [2048, 5632], P('dp', 'tensor')
- down_weight_grad: float32 [5632, 2048], P('tensor', 'dp')
The draws below stay inside these ranges and needn't reach their ends.
Inputs may be any that keep to these rules, and one draw needn't show every extreme that they name: `active`: exactly one of the 6 slots is 0, the others are 1. Slot j of micro-batch m holds sequence assignment[m * 2 + j]; every sequence is in one slot.
All inputs are finite; a program needn't handle non-finite values.
Results may differ from the reference program's by a relative error of at most 0.018.
Values may be sent and summed in bfloat16 or wider, within the bound.
No kernel may reach another device: no remote copies, remote signals or barrier semaphores. Data moves between devices by JAX's collectives and lax.ppermute only.
A program may use at most 320 MiB of HBM per device.

```python
import jax
import jax.numpy as jnp
from jax import lax

D = 2048
H = 16
KVH = 4
HD = 128
FF = 5632
SEQ_DEV = 64
KEY_BLOCK = 512
NMB = 3
SEQ_MB = 2
NSEQ = 6
SEQLEN = 1024
N_DP = 16


def draw_active(key, part):
    key = jax.random.fold_in(key, 3)
    skipped = jax.random.randint(key, (), 0, NMB * SEQ_MB)
    slots = jnp.arange(NMB * SEQ_MB, dtype=jnp.int32)
    return (slots != skipped).astype(jnp.int32).reshape(NMB, SEQ_MB)


def with_spikes(values, stream_key, source, target, shards_of, factor):
    owner, partner = [(jnp.arange(values.shape[axis_at]) // (values.shape[axis_at] // shards_of)).reshape([-1 if axis == axis_at else 1 for axis in range(values.ndim)]) for axis_at in (source, target)]
    chosen = jax.random.permutation(stream_key, shards_of)[partner]
    strong = (owner == chosen) | (owner == (partner + shards_of // 2) % shards_of)
    return jnp.where(strong, factor * values, values)


def level_of(key, extent, pieces, low, top_value):
    loudness, own = 1.0, jax.random.fold_in(key, 6)
    for axis_at, shards_of in pieces:
        steps = jnp.exp(jax.random.uniform(jax.random.fold_in(own, axis_at), (shards_of,), jnp.float32, low / len(pieces), top_value / len(pieces)))
        loudness = loudness * jnp.repeat(steps, extent[axis_at] // shards_of).reshape([-1 if axis == axis_at else 1 for axis in range(len(extent))])
    return loudness


def centred(key, extent, spread, reach, cuts=(), kind=jnp.bfloat16):
    gain = level_of(key, extent, cuts, -0.22, 0.18) if cuts else 1.0
    values = jax.random.normal(key, extent, jnp.float32) * spread * gain
    return jnp.minimum(jnp.maximum(values, -reach), reach).astype(kind)


def gaussian_with(rng, dims, scale, reach, shards, heavy, held_as=jnp.bfloat16):
    entries = scale * jax.random.normal(rng, dims, jnp.float32)
    if shards:
        entries = entries * level_of(rng, dims, shards, -0.22, 0.18)
    return jnp.clip(with_spikes(entries, jax.random.fold_in(rng, 3), *heavy), -reach, reach).astype(held_as)


def setup_inputs(seed: int = 0) -> dict:
    seeds = jax.random.split(jax.random.key(seed), 14)
    tokens = gaussian_with(seeds[0], (NSEQ, SEQLEN, D), 1.0, 6.0, ((1, 16),), (1, 2, 16, 2.0))
    cotangent = gaussian_with(seeds[1], (NSEQ, SEQLEN, D), 1.0, 6.0, ((1, 16),), (1, 2, 16, 2.0))
    active = draw_active(jax.random.fold_in(seeds[13], 71), 0)
    assignment = jax.random.permutation(seeds[3], NSEQ).astype(jnp.int32)
    attention_gain = jnp.clip(1.0 + 0.18 * jax.random.normal(seeds[4], (D,), jnp.float32), 0.099609375, 1.8984375).astype(jnp.bfloat16)
    query_weight = centred(seeds[5], (D, H * HD), (D // 2) ** -0.5, 0.1875, ((0, 16), (1, 2)))
    key_weight = centred(seeds[6], (D, KVH * HD), D ** -0.5, 0.125, ((0, 16), (1, 2)))
    value_weight = centred(seeds[7], (D, KVH * HD), D ** -0.5, 0.125, ((0, 16), (1, 2)))
    out_weight = centred(seeds[8], (H * HD, D), (max(1, 4 * H * HD // (SEQ_DEV * N_DP))) ** -0.5, 2.0, ((0, 2), (1, 16)))
    feedforward_gain = jnp.clip(1.0 + 0.18 * jax.random.normal(seeds[9], (D,), jnp.float32), 0.099609375, 1.8984375).astype(jnp.bfloat16)
    gate_weight = centred(seeds[10], (D, FF), D ** -0.5, 0.125, ((0, 16), (1, 2)))
    up_weight = centred(seeds[11], (D, FF), D ** -0.5, 0.125, ((0, 16), (1, 2)))
    down_weight = centred(seeds[12], (FF, D), (FF // 2) ** -0.5, 0.109375, ((0, 2), (1, 16)))
    return {"tokens": tokens, "cotangent": cotangent, "active": active, "assignment": assignment, "attention_gain": attention_gain, "query_weight": query_weight, "key_weight": key_weight, "value_weight": value_weight, "out_weight": out_weight, "feedforward_gain": feedforward_gain, "gate_weight": gate_weight, "up_weight": up_weight, "down_weight": down_weight}


@jax.custom_vjp
def low(v):
    return lax.optimization_barrier(v.astype(jnp.bfloat16)).astype(jnp.float32)

@jax.custom_vjp
def low_back(v):
    return v

def low_keep(v):
    return (low(v), None)

def low_pass(kept, grad):
    return (grad,)

def back_keep(v):
    return (v, None)

def back_low(kept, grad):
    return (low(grad),)
low.defvjp(low_keep, low_pass)
low_back.defvjp(back_keep, back_low)
EPSILON = 1e-05
NEGATIVE = -1e+30
HIGHEST_MODE = lax.Precision.HIGHEST

def rms_scale(values):
    return lax.rsqrt(lax.optimization_barrier(jnp.mean(values * values, axis=-1, keepdims=True)) + EPSILON)

def rotary_tables(positions):
    half_width = HD // 2
    frequency = jnp.exp(-jnp.log(10000.0) * (2.0 * jnp.arange(half_width, dtype=jnp.float32) / HD))
    angles = positions.astype(jnp.float32)[:, None] * frequency[None, :]
    return (jnp.cos(angles), jnp.sin(angles))

def rotate(values, cosine_table, sine_table):
    half_width = HD // 2
    first_half = values[..., :half_width]
    second_half = values[..., half_width:]
    cosine_part = cosine_table[:, None, :]
    sine_part = sine_table[:, None, :]
    return jnp.concatenate([first_half * cosine_part - second_half * sine_part, second_half * cosine_part + first_half * sine_part], axis=-1)

def one_sequence(token_rows, live_scale, params):
    attention_gain, query_weight, key_weight, value_weight, out_weight, feedforward_gain, gate_weight, up_weight, down_weight = params
    group_size = H // KVH
    hidden = low(token_rows * rms_scale(token_rows) * attention_gain)
    cosine_table, sine_table = rotary_tables(jnp.arange(SEQLEN, dtype=jnp.int32))
    query_raw = low_back(jnp.dot(hidden, query_weight, precision=HIGHEST_MODE))
    key_raw = low_back(jnp.dot(hidden, key_weight, precision=HIGHEST_MODE))
    value_raw = low_back(jnp.dot(hidden, value_weight, precision=HIGHEST_MODE))
    queries = low(rotate(query_raw.reshape(SEQLEN, H, HD), cosine_table, sine_table))
    keys_all = low(rotate(key_raw.reshape(SEQLEN, KVH, HD), cosine_table, sine_table))
    values_all = low(value_raw.reshape(SEQLEN, KVH, HD))
    grouped = queries.reshape(SEQLEN // KEY_BLOCK, KEY_BLOCK, KVH, group_size, HD)
    block_starts = jnp.arange(SEQLEN // KEY_BLOCK, dtype=jnp.int32) * KEY_BLOCK

    def attend(pair):
        query_block, block_start = pair
        scores = jnp.einsum('qkgd,tkd->kgqt', query_block, keys_all, precision=HIGHEST_MODE) * HD ** (-0.5)
        scores = low_back(scores)
        allowed = (block_start + jnp.arange(KEY_BLOCK, dtype=jnp.int32))[:, None] >= jnp.arange(SEQLEN, dtype=jnp.int32)[None, :]
        scores = jnp.where(allowed[None, None], scores, NEGATIVE)
        row_top = lax.optimization_barrier(jnp.max(scores, axis=-1, keepdims=True))
        exponent = jnp.exp(scores - row_top)
        soft_block = exponent / lax.optimization_barrier(jnp.sum(exponent, axis=-1, keepdims=True))
        return jnp.einsum('kgqt,tkd->qkgd', low(soft_block), values_all, precision=HIGHEST_MODE)
    attended = lax.map(jax.checkpoint(attend), (grouped, block_starts))
    mixed_out = low(low_back(attended.reshape(SEQLEN, H * HD)))
    branch = low_back(jnp.dot(mixed_out, out_weight, precision=HIGHEST_MODE))
    middle = token_rows + live_scale * branch
    hidden_mlp = low(middle * rms_scale(middle) * feedforward_gain)
    gate_values = low_back(jnp.dot(hidden_mlp, gate_weight, precision=HIGHEST_MODE))
    up_values = low_back(jnp.dot(hidden_mlp, up_weight, precision=HIGHEST_MODE))
    product = low(gate_values * jax.nn.sigmoid(gate_values) * up_values)
    down_values = low_back(jnp.dot(product, down_weight, precision=HIGHEST_MODE))
    return middle + live_scale * down_values

def reference(tokens, cotangent, active, assignment, attention_gain, query_weight, key_weight, value_weight, out_weight, feedforward_gain, gate_weight, up_weight, down_weight):
    flat_active = active.reshape(-1).astype(jnp.float32)
    matches = (assignment[:, None] == jnp.arange(NSEQ, dtype=jnp.int32)[None, :]).astype(jnp.float32)
    live = lax.optimization_barrier(jnp.sum(matches * flat_active[:, None], axis=0))
    params = (attention_gain.astype(jnp.float32), query_weight.astype(jnp.float32), key_weight.astype(jnp.float32), value_weight.astype(jnp.float32), out_weight.astype(jnp.float32), feedforward_gain.astype(jnp.float32), gate_weight.astype(jnp.float32), up_weight.astype(jnp.float32), down_weight.astype(jnp.float32))
    token_values = tokens.astype(jnp.float32)

    def forward(token_all, weights_all):

        def per_sequence(pair):
            return one_sequence(pair[0], pair[1], weights_all)
        return lax.map(jax.checkpoint(per_sequence), (token_all, live))
    outputs, pullback = jax.vjp(forward, token_values, params)
    input_grad, weight_grads = pullback(cotangent.astype(jnp.float32))
    return (outputs.astype(jnp.bfloat16), input_grad, weight_grads[0], weight_grads[1], weight_grads[2], weight_grads[3], weight_grads[4], weight_grads[5], weight_grads[6], weight_grads[7], weight_grads[8])
```

```python
import functools

import jax
import jax.numpy as jnp
from jax import lax
from jax.experimental import pallas as pl
from jax.experimental.pallas import tpu as pltpu
from jax.sharding import PartitionSpec as P

HD = 128
EPSILON = 1e-05
NEGATIVE = -1e30
VMEM_LIMIT = 48 * 1024 * 1024

bf16 = jnp.bfloat16
f32 = jnp.float32


def rms_scale(values):
    return lax.rsqrt(jnp.mean(values * values, axis=-1, keepdims=True) + EPSILON)


def dot(a, b, ca, cb):
    return lax.dot_general(a, b, (((ca,), (cb,)), ((), ())), preferred_element_type=f32)


def params(**kwargs):
    return pltpu.CompilerParams(vmem_limit_bytes=VMEM_LIMIT, **kwargs)


def turn(v, cosine, sine):
    return v * cosine + pltpu.roll(v, HD // 2, 1) * sine


def rope_kernel(q_cols, k_cols, raw_ref, cos_ref, sin_ref, q_ref, kv_ref):
    cosine, sine = cos_ref[...], sin_ref[...]
    for c in range(0, q_cols, HD):
        q_ref[:, c : c + HD] = turn(raw_ref[:, c : c + HD], cosine, sine).astype(bf16)
    for c in range(0, k_cols, HD):
        v = raw_ref[:, q_cols + c : q_cols + c + HD]
        kv_ref[:, c : c + HD] = turn(v, cosine, sine).astype(bf16)
    kv_ref[:, k_cols:] = raw_ref[:, q_cols + k_cols :].astype(bf16)


def rope(raw, cosine, sine, rows, q_cols, k_cols):
    total = raw.shape[0]
    width = raw.shape[1]
    table = pl.BlockSpec((rows, HD), lambda i: (0, 0))
    return pl.pallas_call(
        functools.partial(rope_kernel, q_cols, k_cols),
        grid=(total // rows,),
        in_specs=[pl.BlockSpec((rows, width), lambda i: (i, 0)), table, table],
        out_specs=[
            pl.BlockSpec((rows, q_cols), lambda i: (i, 0)),
            pl.BlockSpec((rows, 2 * k_cols), lambda i: (i, 0)),
        ],
        out_shape=[
            jax.ShapeDtypeStruct((total, q_cols), bf16),
            jax.ShapeDtypeStruct((total, 2 * k_cols), bf16),
        ],
        compiler_params=params(),
        name="rope",
    )(raw, cosine, sine)


def heads_to_rows(block, kv, group):
    return jnp.concatenate(
        [block[:, (kv * group + g) * HD : (kv * group + g + 1) * HD] for g in range(group)], axis=0
    )


def keys_of(near_ref, far_ref, c):
    parts = [r[:, 0, :, c : c + HD].reshape(-1, HD) for r in (near_ref, far_ref)]
    return jnp.concatenate(parts, axis=0)


def attend_kernel(local_kv, group, q_ref, near_ref, far_ref, qpos_ref, kpos_ref, out_ref, log_ref):
    rows = q_ref.shape[0]
    allowed = kpos_ref[...] <= qpos_ref[...]
    for kv in range(local_kv):
        q = heads_to_rows(q_ref, kv, group)
        keys = keys_of(near_ref, far_ref, kv * HD)
        values = keys_of(near_ref, far_ref, (local_kv + kv) * HD)
        s = jnp.where(allowed, dot(q, keys, 1, 1) * (HD**-0.5), NEGATIVE)
        top = jnp.max(s, axis=-1, keepdims=True)
        e = jnp.exp(s - top)
        total = jnp.sum(e, axis=-1, keepdims=True)
        probs = (e * (1.0 / total)).astype(bf16)
        out = dot(probs, values, 1, 0)
        for g in range(group):
            c = (kv * group + g) * HD
            out_ref[:, c : c + HD] = out[g * rows : (g + 1) * rows].astype(bf16)
        log_ref[kv] = top + jnp.log(total)


def attend(q, near, far, qpos, kpos, rows, local_kv, group):
    total, width = q.shape
    seqs = total // rows
    blocks, _, _, kv_width = near.shape
    kv_spec = pl.BlockSpec((blocks, 1, rows, kv_width), lambda i: (0, i, 0, 0))
    return pl.pallas_call(
        functools.partial(attend_kernel, local_kv, group),
        grid=(seqs,),
        in_specs=[
            pl.BlockSpec((rows, width), lambda i: (i, 0)),
            kv_spec,
            kv_spec,
            pl.BlockSpec(qpos.shape, lambda i: (0, 0)),
            pl.BlockSpec(kpos.shape, lambda i: (0, 0)),
        ],
        out_specs=[
            pl.BlockSpec((rows, width), lambda i: (i, 0)),
            pl.BlockSpec((local_kv, group * rows, 1), lambda i: (i, 0, 0)),
        ],
        out_shape=[
            jax.ShapeDtypeStruct((total, width), bf16),
            jax.ShapeDtypeStruct((seqs * local_kv, group * rows, 1), f32),
        ],
        compiler_params=params(),
        name="attend",
    )(q, near, far, qpos, kpos)


def attend_back_kernel(
    local_kv, group, q_ref, near_ref, far_ref, qpos_ref, kpos_ref, log_ref, grad_ref, cos_ref, sin_ref,
    dq_ref, dnear_ref, dfar_ref,
):
    rows = q_ref.shape[0]
    half = near_ref.shape[0] * rows
    scale = HD**-0.5
    allowed = kpos_ref[...] <= qpos_ref[...]
    cosine, sine = cos_ref[...], sin_ref[...]
    for kv in range(local_kv):
        ck, cv = kv * HD, (local_kv + kv) * HD
        q = heads_to_rows(q_ref, kv, group)
        grad = heads_to_rows(grad_ref, kv, group)
        keys = keys_of(near_ref, far_ref, ck)
        values = keys_of(near_ref, far_ref, cv)
        s = jnp.where(allowed, dot(q, keys, 1, 1) * scale, NEGATIVE)
        probs = jnp.exp(s - log_ref[kv])
        prob_grad = dot(grad, values, 1, 1)
        both = probs * prob_grad
        delta = jnp.sum(both, axis=-1, keepdims=True)
        ds = (both - probs * delta).astype(bf16)
        dq = dot(ds, keys, 1, 0) * scale
        for g in range(group):
            c = (kv * group + g) * HD
            dq_ref[:, c : c + HD] = turn(dq[g * rows : (g + 1) * rows], cosine, -sine).astype(bf16)
        dk = (dot(ds, q, 0, 0) * scale).astype(bf16)
        dv = dot(probs.astype(bf16), grad, 0, 0).astype(bf16)
        for d, c in ((dk, ck), (dv, cv)):
            dnear_ref[:, 0, :, c : c + HD] = d[:half].reshape(-1, rows, HD)
            dfar_ref[:, 0, :, c : c + HD] = d[half:].reshape(-1, rows, HD)


def attend_back(q, near, far, qpos, kpos, log, grad, cosine, sine, rows, local_kv, group):
    total, width = q.shape
    seqs = total // rows
    blocks, _, _, kv_width = near.shape
    kv_spec = pl.BlockSpec((blocks, 1, rows, kv_width), lambda i: (0, i, 0, 0))
    row_spec = pl.BlockSpec((rows, width), lambda i: (i, 0))
    table = pl.BlockSpec((rows, HD), lambda i: (0, 0))
    return pl.pallas_call(
        functools.partial(attend_back_kernel, local_kv, group),
        grid=(seqs,),
        in_specs=[
            row_spec,
            kv_spec,
            kv_spec,
            pl.BlockSpec(qpos.shape, lambda i: (0, 0)),
            pl.BlockSpec(kpos.shape, lambda i: (0, 0)),
            pl.BlockSpec((local_kv, group * rows, 1), lambda i: (i, 0, 0)),
            row_spec,
            table,
            table,
        ],
        out_specs=[row_spec, kv_spec, kv_spec],
        out_shape=[
            jax.ShapeDtypeStruct((total, width), bf16),
            jax.ShapeDtypeStruct(near.shape, bf16),
            jax.ShapeDtypeStruct(far.shape, bf16),
        ],
        compiler_params=params(),
        name="attend_back",
    )(q, near, far, qpos, kpos, log, grad, cosine, sine)


def arrange_kernel(block, order_ref, a_ref, keep_ref, send_ref):
    half = order_ref.shape[0] // 2
    for j in range(half):
        for out_ref, at in ((keep_ref, j), (send_ref, half + j)):
            start = pl.multiple_of(order_ref[at] * block, block)
            out_ref[:, j * block : (j + 1) * block] = a_ref[:, pl.ds(start, block)]


def arrange(a, order):
    rows, width = a.shape
    count = order.shape[0]
    block = width // count
    if block % 128:
        moved = jnp.take(a.reshape(rows, count, block), order, axis=1).reshape(rows, width)
        return moved[:, : width // 2], moved[:, width // 2 :]
    out = jax.ShapeDtypeStruct((rows, width // 2), a.dtype)
    return pl.pallas_call(
        functools.partial(arrange_kernel, block),
        in_specs=[
            pl.BlockSpec(memory_space=pltpu.SMEM),
            pl.BlockSpec(memory_space=pltpu.VMEM),
        ],
        out_specs=[pl.BlockSpec(memory_space=pltpu.VMEM)] * 2,
        out_shape=[out, out],
        compiler_params=params(),
        name="arrange",
    )(order, a)


def local(
    n_dp,
    tokens,
    cotangent,
    active,
    assignment,
    attention_gain,
    query_weight,
    key_weight,
    value_weight,
    out_weight,
    feedforward_gain,
    gate_weight,
    up_weight,
    down_weight,
):
    rows, width = tokens.shape[1:]
    live_seqs = tokens.shape[0] - 1
    total = live_seqs * rows
    block = width // n_dp
    groups = n_dp // 4
    q_cols, k_cols = query_weight.shape[1], key_weight.shape[1]
    hidden_units = gate_weight.shape[1]
    local_kv = k_cols // HD
    group = q_cols // k_cols
    me = lax.axis_index("dp").astype(jnp.int32)

    def flip(v, bits):
        return lax.ppermute(v, "dp", [(i, i ^ bits) for i in range(n_dp)])

    def tensor_flip(v):
        return lax.ppermute(v, "tensor", [(0, 1), (1, 0)])

    def tensor_total(partial_rows):
        mine = lax.optimization_barrier(partial_rows.astype(bf16))
        return mine.astype(f32) + tensor_flip(mine).astype(f32)

    near_places = [far * 4 + pair * 2 for pair in range(2) for far in range(groups)]
    places = near_places + [place + 1 for place in near_places]
    owners = jnp.bitwise_xor(me, jnp.asarray(places, jnp.int32))

    positions = me * rows + jnp.arange(rows, dtype=jnp.int32)
    frequency = jnp.exp(
        -jnp.log(10000.0) * (2.0 * jnp.arange(HD // 2, dtype=f32) / HD)
    )
    angles = positions.astype(f32)[:, None] * frequency[None, :]
    cosine = jnp.concatenate([jnp.cos(angles)] * 2, axis=1)
    sine = jnp.concatenate([-jnp.sin(angles), jnp.sin(angles)], axis=1)
    qpos = jnp.tile(positions, group)[:, None]
    kpos = (owners[:, None] * rows + jnp.arange(rows, dtype=jnp.int32)[None, :]).reshape(1, -1)

    gains = jnp.stack([attention_gain, feedforward_gain], axis=1)
    gains = jnp.pad(gains, ((0, 0), (0, 126)))
    first = lax.all_gather(
        jnp.concatenate([query_weight, key_weight, value_weight, out_weight.T, gains], axis=1),
        "dp", axis=0, tiled=True,
    )
    second = lax.all_gather(
        jnp.concatenate([gate_weight, up_weight], axis=1), "dp", axis=0, tiled=True
    )
    down_turned = lax.all_gather(down_weight.T, "dp", axis=0, tiled=True)
    qkv_cols = q_cols + 2 * k_cols
    qkv_full = first[:, :qkv_cols]
    out_turned = first[:, qkv_cols : qkv_cols + q_cols]
    gain_attn = first[:, qkv_cols + q_cols].astype(f32)[None, :]
    gain_mlp = first[:, qkv_cols + q_cols + 1].astype(f32)[None, :]

    dead_slot = jnp.argmin(active.reshape(-1))
    dead = assignment[dead_slot]
    is_dead = (jnp.arange(live_seqs, dtype=jnp.int32) == dead)[:, None, None]

    def pick(v):
        return jnp.where(is_dead, v[live_seqs:], v[:live_seqs]).reshape(total, width)

    def unpick(live_values, skipped):
        live_values = live_values.reshape(live_seqs, rows, width)
        last = lax.dynamic_slice_in_dim(live_values, jnp.minimum(dead, live_seqs - 1), 1, 0)
        return jnp.concatenate(
            [
                jnp.where(is_dead, skipped[:live_seqs], live_values),
                jnp.where(dead == live_seqs, skipped[live_seqs:], last),
            ],
            axis=0,
        )

    token_rows = pick(tokens).astype(f32)
    down_grad = lax.optimization_barrier(pick(cotangent))
    upstream = down_grad.astype(f32)

    attn_scale = rms_scale(token_rows)
    hidden = (token_rows * attn_scale * gain_attn).astype(bf16)
    qkv_raw = dot(hidden, qkv_full, 1, 0)
    queries, kv_own = rope(qkv_raw, cosine, sine, rows, q_cols, k_cols)
    kv_own = kv_own.reshape(1, live_seqs, rows, 2 * k_cols)
    kv_far = jnp.concatenate([kv_own] + [flip(kv_own, 4 * k) for k in range(1, groups)], axis=0)
    kv_near = jnp.concatenate([kv_far, flip(kv_far, 2)], axis=0)
    kv_other = flip(kv_near, 1)
    mixed_out, log_total = attend(
        queries, kv_near, kv_other, qpos, kpos, rows, local_kv, group
    )
    branch = tensor_total(dot(mixed_out, out_turned, 1, 1))
    middle = token_rows + branch

    mlp_scale = rms_scale(middle)
    normed_mlp = middle * mlp_scale
    hidden_mlp = (normed_mlp * gain_mlp).astype(bf16)
    gate_up = dot(hidden_mlp, second, 1, 0)
    gate_values, up_values = gate_up[:, :hidden_units], gate_up[:, hidden_units:]
    sigmoid_gate = jax.nn.sigmoid(gate_values)
    silu_gate = gate_values * sigmoid_gate
    product = (silu_gate * up_values).astype(bf16)

    def side(a):
        keep, send = arrange(a, owners)
        return jnp.concatenate([keep, flip(send, 1)], axis=0)

    def both_cores(b):
        return jnp.concatenate([b, flip(b, 1)], axis=0)

    def summed(a_side, b):
        half = groups * block
        sent = dot(a_side[:, half:], b, 0, 0).astype(bf16)
        kept = dot(a_side[:, :half], b, 0, 0)
        pair = (kept + flip(sent, 2).astype(f32)).reshape(groups, block, b.shape[1])
        out = pair[0]
        for k in range(1, groups):
            out = out + flip(pair[k].astype(bf16), 4 * k).astype(f32)
        return out

    grad_down = summed(side(down_grad), both_cores(product)).T
    down_values = tensor_total(dot(product, down_turned, 1, 1))
    result = unpick((middle + down_values).astype(bf16), tokens)

    product_grad = dot(down_grad, down_turned, 1, 0)
    gate_grad = (
        product_grad * up_values * (sigmoid_gate * (1.0 + gate_values * (1.0 - sigmoid_gate)))
    ).astype(bf16)
    up_grad = (product_grad * silu_gate).astype(bf16)
    gate_up_grad = jnp.concatenate([gate_grad, up_grad], axis=1)
    mlp_side = side(hidden_mlp)
    grad_gate = summed(mlp_side, both_cores(gate_grad))
    grad_up = summed(mlp_side, both_cores(up_grad))
    hidden_mlp_grad = tensor_total(dot(gate_up_grad, second, 1, 1))
    gain_mlp_rows = jnp.sum(hidden_mlp_grad * normed_mlp, axis=0)
    normed_grad = hidden_mlp_grad * gain_mlp
    middle_grad = upstream + mlp_scale * (
        normed_grad - normed_mlp * jnp.mean(normed_grad * normed_mlp, axis=-1, keepdims=True)
    )

    branch_grad = middle_grad.astype(bf16)
    grad_out = summed(side(branch_grad), both_cores(mixed_out)).T
    mixed_grad = dot(branch_grad, out_turned, 1, 0).astype(bf16)
    query_grad, dkv_near, dkv_other = attend_back(
        queries, kv_near, kv_other, qpos, kpos, log_total, mixed_grad, cosine, sine,
        rows, local_kv, group,
    )
    dkv_near = dkv_near.astype(f32) + flip(dkv_other, 1).astype(f32)
    dkv_far = dkv_near[:groups] + flip(dkv_near[groups:].astype(bf16), 2).astype(f32)
    dkv = dkv_far[0]
    for k in range(1, groups):
        dkv = dkv + flip(dkv_far[k].astype(bf16), 4 * k).astype(f32)
    dkv = dkv.reshape(total, 2 * k_cols)
    key_grad, _ = rope(
        jnp.concatenate([dkv[:, :k_cols], dkv], axis=1), cosine, -sine, rows, k_cols, k_cols
    )
    qkv_grad = jnp.concatenate([query_grad, key_grad, dkv[:, k_cols:].astype(bf16)], axis=1)
    grad_qkv = summed(side(hidden), both_cores(qkv_grad))
    hidden_grad = tensor_total(dot(qkv_grad, qkv_full, 1, 1))
    normed_attn = token_rows * attn_scale
    gain_attn_rows = jnp.sum(hidden_grad * normed_attn, axis=0)
    normed_attn_grad = hidden_grad * gain_attn
    input_grad = middle_grad + attn_scale * (
        normed_attn_grad
        - normed_attn * jnp.mean(normed_attn_grad * normed_attn, axis=-1, keepdims=True)
    )
    input_grad = unpick(input_grad, cotangent.astype(f32))

    gain_rows = jnp.stack([gain_attn_rows, gain_mlp_rows]).reshape(2, n_dp, block)
    gain_rows = jnp.take(gain_rows, owners, axis=1)
    gain_rows = gain_rows[:, : 2 * groups] + flip(gain_rows[:, 2 * groups :], 1)
    gain_rows = gain_rows[:, :groups] + flip(gain_rows[:, groups:], 2)
    gain_own = gain_rows[:, 0]
    for k in range(1, groups):
        gain_own = gain_own + flip(gain_rows[:, k], 4 * k)

    return (
        result,
        input_grad,
        gain_own[0],
        grad_qkv[:, :q_cols],
        grad_qkv[:, q_cols : q_cols + k_cols],
        grad_qkv[:, q_cols + k_cols :],
        grad_out,
        gain_own[1],
        grad_gate,
        grad_up,
        grad_down,
    )


def solution(mesh):
    rows = P(None, "dp", None)
    split = P("dp", "tensor")
    turned = P("tensor", "dp")
    gain = P("dp")
    weights = (gain, split, split, split, turned, gain, split, split, turned)
    return jax.shard_map(
        functools.partial(local, mesh.shape["dp"]),
        mesh=mesh,
        in_specs=(rows, rows, P(), P(), *weights),
        out_specs=(rows, rows, *weights),
        check_vma=False,
    )
```

```python
import functools
import math

import jax
import jax.numpy as jnp
from jax import lax
from jax.experimental import pallas as pl
from jax.experimental.pallas import tpu as pltpu
from jax.sharding import PartitionSpec as P

HD = 128
EPSILON = 1e-05
NEGATIVE = -1e30
VMEM_LIMIT = 48 * 1024 * 1024

HINT = pl.CostEstimate(flops=1, bytes_accessed=1, transcendentals=0)

bf16 = jnp.bfloat16
f32 = jnp.float32


def rms_scale(values):
    return lax.rsqrt(jnp.mean(values * values, axis=-1, keepdims=True) + EPSILON)


def dot(a, b, ca, cb):
    return lax.dot_general(a, b, (((ca,), (cb,)), ((), ())), preferred_element_type=f32)


def params(**kwargs):
    return pltpu.CompilerParams(vmem_limit_bytes=VMEM_LIMIT, **kwargs)


def turn(v, cosine, sine):
    return v * cosine + pltpu.roll(v, HD // 2, 1) * sine


def first_tiles(arrays):
    return [v[(0,) * (v.ndim - 2)][:16, :128] for v in arrays]


def unread(others):
    return [pl.BlockSpec(memory_space=pl.ANY)] * len(others)


def rope_kernel(q_cols, k_cols, raw_ref, cos_ref, sin_ref, *refs):
    q_ref, kv_ref = refs[-2:]
    cosine, sine = cos_ref[...], sin_ref[...]
    for c in range(0, q_cols, HD):
        q_ref[:, c : c + HD] = turn(raw_ref[:, c : c + HD], cosine, sine).astype(bf16)
    for c in range(0, k_cols, HD):
        v = raw_ref[:, q_cols + c : q_cols + c + HD]
        kv_ref[:, c : c + HD] = turn(v, cosine, sine).astype(bf16)
    kv_ref[:, k_cols:] = raw_ref[:, q_cols + k_cols :].astype(bf16)


def rope(raw, cosine, sine, rows, q_cols, k_cols, others=()):
    total = raw.shape[0]
    width = raw.shape[1]
    table = pl.BlockSpec((rows, HD), lambda i: (0, 0))
    return pl.pallas_call(
        functools.partial(rope_kernel, q_cols, k_cols),
        grid=(total // rows,),
        in_specs=[pl.BlockSpec((rows, width), lambda i: (i, 0)), table, table, *unread(others)],
        out_specs=[
            pl.BlockSpec((rows, q_cols), lambda i: (i, 0)),
            pl.BlockSpec((rows, 2 * k_cols), lambda i: (i, 0)),
        ],
        out_shape=[
            jax.ShapeDtypeStruct((total, q_cols), bf16),
            jax.ShapeDtypeStruct((total, 2 * k_cols), bf16),
        ],
        compiler_params=params(),
        cost_estimate=HINT,
        name="rope",
    )(raw, cosine, sine, *first_tiles(others))


def heads_to_rows(block, kv, group):
    return jnp.concatenate(
        [block[:, (kv * group + g) * HD : (kv * group + g + 1) * HD] for g in range(group)], axis=0
    )


def keys_of(near_ref, far_ref, c):
    parts = [r[:, 0, :, c : c + HD].reshape(-1, HD) for r in (near_ref, far_ref)]
    return jnp.concatenate(parts, axis=0)


def attend_kernel(local_kv, group, q_ref, near_ref, far_ref, qpos_ref, kpos_ref, out_ref, log_ref):
    rows = q_ref.shape[0]
    allowed = kpos_ref[...] <= qpos_ref[...]
    for kv in range(local_kv):
        q = heads_to_rows(q_ref, kv, group)
        keys = keys_of(near_ref, far_ref, kv * HD)
        values = keys_of(near_ref, far_ref, (local_kv + kv) * HD)
        s = jnp.where(allowed, dot(q, keys, 1, 1) * (HD**-0.5), NEGATIVE)
        top = jnp.max(s, axis=-1, keepdims=True)
        e = jnp.exp(s - top)
        total = jnp.sum(e, axis=-1, keepdims=True)
        probs = (e * (1.0 / total)).astype(bf16)
        out = dot(probs, values, 1, 0)
        for g in range(group):
            c = (kv * group + g) * HD
            out_ref[:, c : c + HD] = out[g * rows : (g + 1) * rows].astype(bf16)
        log_ref[kv] = top + jnp.log(total)


def attend(q, near, far, qpos, kpos, rows, local_kv, group):
    total, width = q.shape
    seqs = total // rows
    blocks, _, _, kv_width = near.shape
    kv_spec = pl.BlockSpec((blocks, 1, rows, kv_width), lambda i: (0, i, 0, 0))
    return pl.pallas_call(
        functools.partial(attend_kernel, local_kv, group),
        grid=(seqs,),
        in_specs=[
            pl.BlockSpec((rows, width), lambda i: (i, 0)),
            kv_spec,
            kv_spec,
            pl.BlockSpec(qpos.shape, lambda i: (0, 0)),
            pl.BlockSpec(kpos.shape, lambda i: (0, 0)),
        ],
        out_specs=[
            pl.BlockSpec((rows, width), lambda i: (i, 0)),
            pl.BlockSpec((local_kv, group * rows, 1), lambda i: (i, 0, 0)),
        ],
        out_shape=[
            jax.ShapeDtypeStruct((total, width), bf16),
            jax.ShapeDtypeStruct((seqs * local_kv, group * rows, 1), f32),
        ],
        compiler_params=params(),
        cost_estimate=HINT,
        name="attend",
    )(q, near, far, qpos, kpos)


def attend_back_kernel(
    local_kv, group, q_ref, near_ref, far_ref, qpos_ref, kpos_ref, log_ref, grad_ref, cos_ref, sin_ref,
    *refs,
):
    dq_ref, dnear_ref, dfar_ref = refs[-3:]
    rows = q_ref.shape[0]
    half = near_ref.shape[0] * rows
    scale = HD**-0.5
    allowed = kpos_ref[...] <= qpos_ref[...]
    cosine, sine = cos_ref[...], sin_ref[...]
    for kv in range(local_kv):
        ck, cv = kv * HD, (local_kv + kv) * HD
        q = heads_to_rows(q_ref, kv, group)
        grad = heads_to_rows(grad_ref, kv, group)
        keys = keys_of(near_ref, far_ref, ck)
        values = keys_of(near_ref, far_ref, cv)
        s = jnp.where(allowed, dot(q, keys, 1, 1) * scale, NEGATIVE)
        probs = jnp.exp(s - log_ref[kv])
        prob_grad = dot(grad, values, 1, 1)
        both = probs * prob_grad
        delta = jnp.sum(both, axis=-1, keepdims=True)
        ds = (both - probs * delta).astype(bf16)
        dq = dot(ds, keys, 1, 0) * scale
        for g in range(group):
            c = (kv * group + g) * HD
            dq_ref[:, c : c + HD] = turn(dq[g * rows : (g + 1) * rows], cosine, -sine).astype(bf16)
        dk = (dot(ds, q, 0, 0) * scale).astype(bf16)
        dv = dot(probs.astype(bf16), grad, 0, 0).astype(bf16)
        for d, c in ((dk, ck), (dv, cv)):
            dnear_ref[:, 0, :, c : c + HD] = d[:half].reshape(-1, rows, HD)
            dfar_ref[:, 0, :, c : c + HD] = d[half:].reshape(-1, rows, HD)


def attend_back(
    q, near, far, qpos, kpos, log, grad, cosine, sine, rows, local_kv, group, others
):
    total, width = q.shape
    seqs = total // rows
    blocks, _, _, kv_width = near.shape
    kv_spec = pl.BlockSpec((blocks, 1, rows, kv_width), lambda i: (0, i, 0, 0))
    row_spec = pl.BlockSpec((rows, width), lambda i: (i, 0))
    table = pl.BlockSpec((rows, HD), lambda i: (0, 0))
    return pl.pallas_call(
        functools.partial(attend_back_kernel, local_kv, group),
        grid=(seqs,),
        in_specs=[
            row_spec,
            kv_spec,
            kv_spec,
            pl.BlockSpec(qpos.shape, lambda i: (0, 0)),
            pl.BlockSpec(kpos.shape, lambda i: (0, 0)),
            pl.BlockSpec((local_kv, group * rows, 1), lambda i: (i, 0, 0)),
            row_spec,
            table,
            table,
            *unread(others),
        ],
        out_specs=[row_spec, kv_spec, kv_spec],
        out_shape=[
            jax.ShapeDtypeStruct((total, width), bf16),
            jax.ShapeDtypeStruct(near.shape, bf16),
            jax.ShapeDtypeStruct(far.shape, bf16),
        ],
        compiler_params=params(),
        cost_estimate=HINT,
        name="attend_back",
    )(q, near, far, qpos, kpos, log, grad, cosine, sine, *first_tiles(others))


def arrange_kernel(block, order_ref, a_ref, keep_ref, send_ref):
    half = order_ref.shape[0] // 2
    for j in range(half):
        for out_ref, at in ((keep_ref, j), (send_ref, half + j)):
            start = pl.multiple_of(order_ref[at] * block, block)
            out_ref[:, j * block : (j + 1) * block] = a_ref[:, pl.ds(start, block)]


def arrange(a, order):
    rows, width = a.shape
    count = order.shape[0]
    block = width // count
    if block % 128:
        moved = jnp.take(a.reshape(rows, count, block), order, axis=1).reshape(rows, width)
        return moved[:, : width // 2], moved[:, width // 2 :]
    out = jax.ShapeDtypeStruct((rows, width // 2), a.dtype)
    return pl.pallas_call(
        functools.partial(arrange_kernel, block),
        in_specs=[
            pl.BlockSpec(memory_space=pltpu.SMEM),
            pl.BlockSpec(memory_space=pltpu.VMEM),
        ],
        out_specs=[pl.BlockSpec(memory_space=pltpu.VMEM)] * 2,
        out_shape=[out, out],
        compiler_params=params(),
        cost_estimate=HINT,
        name="arrange",
    )(order, a)


def forward_kernel(hidden_ref, gate_w_ref, up_w_ref, gate_ref, up_ref, product_ref):
    hidden = hidden_ref[...]
    gate = dot(hidden, gate_w_ref[...], 1, 0)
    up = dot(hidden, up_w_ref[...], 1, 0)
    gate_ref[...] = gate
    up_ref[...] = up
    product_ref[...] = (gate * jax.nn.sigmoid(gate) * up).astype(bf16)


def feed_forward(hidden, weights, units):
    rows, width = hidden.shape
    tile = math.gcd(units, 256)
    tiles = units // tile
    whole = pl.BlockSpec((rows, width), lambda i: (0, 0))
    column = pl.BlockSpec((rows, tile), lambda i: (0, i))
    return pl.pallas_call(
        forward_kernel,
        grid=(tiles,),
        in_specs=[
            whole,
            pl.BlockSpec((width, tile), lambda i: (0, i)),
            pl.BlockSpec((width, tile), lambda i: (0, tiles + i)),
        ],
        out_specs=[column] * 3,
        out_shape=[jax.ShapeDtypeStruct((rows, units), t) for t in (f32, f32, bf16)],
        compiler_params=params(),
        cost_estimate=HINT,
        name="feed_forward",
    )(hidden, weights, weights)


def backward_kernel(down_grad_ref, gate_ref, up_ref, gate_w_ref, up_w_ref, down_w_ref, *refs):
    gate_grad_ref, up_grad_ref, partial_ref, sum_ref = refs[-4:]
    product_grad = dot(down_grad_ref[...], down_w_ref[...], 1, 0)
    gate, up = gate_ref[...], up_ref[...]
    sigmoid = jax.nn.sigmoid(gate)
    gate_grad = (product_grad * up * (sigmoid * (1.0 + gate * (1.0 - sigmoid)))).astype(bf16)
    up_grad = (product_grad * gate * sigmoid).astype(bf16)
    gate_grad_ref[...] = gate_grad
    up_grad_ref[...] = up_grad
    term = dot(gate_grad, gate_w_ref[...], 1, 1) + dot(up_grad, up_w_ref[...], 1, 1)

    @pl.when(pl.program_id(0) == 0)
    def _():
        sum_ref[...] = term

    @pl.when(pl.program_id(0) != 0)
    def _():
        sum_ref[...] += term

    @pl.when(pl.program_id(0) == pl.num_programs(0) - 1)
    def _():
        partial_ref[...] = sum_ref[...].astype(bf16)


def feed_forward_back(down_grad, gate, up, weights, units, others):
    rows, width = down_grad.shape
    tile = math.gcd(units, 256)
    tiles = units // tile
    whole = pl.BlockSpec((rows, width), lambda i: (0, 0))
    column = pl.BlockSpec((rows, tile), lambda i: (0, i))
    return pl.pallas_call(
        backward_kernel,
        grid=(tiles,),
        in_specs=[
            whole,
            column,
            column,
            pl.BlockSpec((width, tile), lambda i: (0, i)),
            pl.BlockSpec((width, tile), lambda i: (0, tiles + i)),
            pl.BlockSpec((width, tile), lambda i: (0, 2 * tiles + i)),
        ]
        + unread(others),
        out_specs=[column, column, whole],
        out_shape=[
            jax.ShapeDtypeStruct((rows, units), bf16),
            jax.ShapeDtypeStruct((rows, units), bf16),
            jax.ShapeDtypeStruct((rows, width), bf16),
        ],
        scratch_shapes=[pltpu.VMEM((rows, width), f32)],
        compiler_params=params(),
        cost_estimate=HINT,
        name="feed_forward_back",
    )(down_grad, gate, up, weights, weights, weights, *first_tiles(others))


def product_kernel(extra, *refs):
    a_ref, a2_ref, b_ref, b2_ref = refs[:4]
    out_ref, turned_ref = refs[-2:]

    @pl.when(pl.program_id(0) == 0)
    def _():
        turned_ref[...] = jnp.concatenate([a_ref[...], a2_ref[...]], axis=0).T

    b = jnp.concatenate([b_ref[...], b2_ref[...]], axis=0)
    out = dot(turned_ref[...], b, 1, 0)
    if extra:
        out = out + refs[4][...].astype(f32)
    out_ref[...] = out.astype(bf16)


def side_product(side, half, b, b2, columns, added=None, others=()):
    a, a2 = side
    rows = a.shape[0]
    height = a.shape[1] // 2
    start, count = columns
    tile = math.gcd(math.gcd(start, count), 256)
    first = start // tile
    a_spec = pl.BlockSpec((rows, height), lambda i: (0, half))
    b_spec = pl.BlockSpec((rows, tile), lambda i: (0, first + i))
    out_spec = pl.BlockSpec((height, tile), lambda i: (0, i))
    extra = [] if added is None else [added]
    return pl.pallas_call(
        functools.partial(product_kernel, len(extra)),
        grid=(count // tile,),
        in_specs=[a_spec, a_spec, b_spec, b_spec]
        + [out_spec] * len(extra)
        + unread(others),
        out_specs=out_spec,
        out_shape=jax.ShapeDtypeStruct((height, count), bf16),
        scratch_shapes=[pltpu.VMEM((height, 2 * rows), bf16)],
        compiler_params=params(),
        cost_estimate=HINT,
        name="side_product",
    )(a, a2, b, b2, *extra, *first_tiles(others))


def norm_back_kernel(mine_ref, theirs_ref, v_ref, gain_ref, base_ref, *refs):
    grad_ref, low_ref, gain_grad_ref = refs[-3:]
    hidden_grad = mine_ref[...].astype(f32) + theirs_ref[...].astype(f32)
    v = v_ref[...].astype(f32)
    scale = rms_scale(v)
    normed = v * scale
    gain_grad = jnp.sum(hidden_grad * normed, axis=0, keepdims=True)

    @pl.when(pl.program_id(0) == 0)
    def _():
        gain_grad_ref[...] = gain_grad

    @pl.when(pl.program_id(0) != 0)
    def _():
        gain_grad_ref[...] += gain_grad

    g = hidden_grad * gain_ref[...]
    out = base_ref[...].astype(f32) + scale * (
        g - normed * jnp.mean(g * normed, axis=-1, keepdims=True)
    )
    grad_ref[...] = out
    low_ref[...] = out.astype(bf16)


def norm_back(mine, theirs, v, gain, base, rows, others=()):
    total, width = mine.shape
    spec = pl.BlockSpec((rows, width), lambda i: (i, 0))
    row = pl.BlockSpec((1, width), lambda i: (0, 0))
    return pl.pallas_call(
        norm_back_kernel,
        grid=(total // rows,),
        in_specs=[spec, spec, spec, row, spec, *unread(others)],
        out_specs=[spec, spec, row],
        out_shape=[
            jax.ShapeDtypeStruct((total, width), f32),
            jax.ShapeDtypeStruct((total, width), bf16),
            jax.ShapeDtypeStruct((1, width), f32),
        ],
        compiler_params=params(),
        cost_estimate=HINT,
        name="norm_back",
    )(mine, theirs, v, gain, base, *first_tiles(others))


def pass_kernel(*refs):
    pass


def after(v, *others):
    spec = pl.BlockSpec(memory_space=pl.ANY)
    return pl.pallas_call(
        pass_kernel,
        in_specs=[spec] * (1 + len(others)),
        out_specs=spec,
        out_shape=jax.ShapeDtypeStruct(v.shape, v.dtype),
        input_output_aliases={0: 0},
        cost_estimate=HINT,
        name="after",
    )(v, *first_tiles(others))


def local(
    n_dp,
    tokens,
    cotangent,
    active,
    assignment,
    attention_gain,
    query_weight,
    key_weight,
    value_weight,
    out_weight,
    feedforward_gain,
    gate_weight,
    up_weight,
    down_weight,
):
    rows, width = tokens.shape[1:]
    live_seqs = tokens.shape[0] - 1
    total = live_seqs * rows
    block = width // n_dp
    groups = n_dp // 4
    q_cols, k_cols = query_weight.shape[1], key_weight.shape[1]
    hidden_units = gate_weight.shape[1]
    local_kv = k_cols // HD
    group = q_cols // k_cols
    me = lax.axis_index("dp").astype(jnp.int32)

    def flip(v, bits):
        return lax.ppermute(v, "dp", [(i, i ^ bits) for i in range(n_dp)])

    def tensor_flip(v):
        return lax.ppermute(v, "tensor", [(0, 1), (1, 0)])

    def tensor_total(partial_rows):
        mine = lax.optimization_barrier(partial_rows.astype(bf16))
        return mine.astype(f32) + tensor_flip(mine).astype(f32)

    far_bits = [1 << b for b in range(groups.bit_length() - 1)]
    fars = [0]
    for bit in reversed(far_bits):
        fars = fars + [far + bit for far in fars]
    near_places = [far * 4 + pair * 2 for pair in range(2) for far in fars]
    places = near_places + [place + 1 for place in near_places]
    owners = jnp.bitwise_xor(me, jnp.asarray(places, jnp.int32))

    positions = me * rows + jnp.arange(rows, dtype=jnp.int32)
    frequency = jnp.exp(
        -jnp.log(10000.0) * (2.0 * jnp.arange(HD // 2, dtype=f32) / HD)
    )
    angles = positions.astype(f32)[:, None] * frequency[None, :]
    cosine = jnp.concatenate([jnp.cos(angles)] * 2, axis=1)
    sine = jnp.concatenate([-jnp.sin(angles), jnp.sin(angles)], axis=1)
    qpos = jnp.tile(positions, group)[:, None]
    kpos = (owners[:, None] * rows + jnp.arange(rows, dtype=jnp.int32)[None, :]).reshape(1, -1)

    gains = jnp.stack([attention_gain, feedforward_gain], axis=1)
    gains = jnp.pad(gains, ((0, 0), (0, 126)))
    first = lax.all_gather(
        jnp.concatenate([query_weight, key_weight, value_weight, out_weight.T, gains], axis=1),
        "dp", axis=0, tiled=True,
    )
    second = lax.all_gather(
        jnp.concatenate([gate_weight, up_weight, down_weight.T], axis=1), "dp", axis=0, tiled=True
    )
    down_turned = second[:, 2 * hidden_units :]
    qkv_cols = q_cols + 2 * k_cols
    qkv_full = first[:, :qkv_cols]
    out_turned = first[:, qkv_cols : qkv_cols + q_cols]
    gain_attn = first[:, qkv_cols + q_cols].astype(f32)[None, :]
    gain_mlp = first[:, qkv_cols + q_cols + 1].astype(f32)[None, :]

    dead_slot = jnp.argmin(active.reshape(-1))
    dead = assignment[dead_slot]
    is_dead = (jnp.arange(live_seqs, dtype=jnp.int32) == dead)[:, None, None]

    def pick(v):
        return jnp.where(is_dead, v[live_seqs:], v[:live_seqs]).reshape(total, width)

    def unpick(live_values, skipped):
        live_values = live_values.reshape(live_seqs, rows, width)
        last = lax.dynamic_slice_in_dim(live_values, jnp.minimum(dead, live_seqs - 1), 1, 0)
        return jnp.concatenate(
            [
                jnp.where(is_dead, skipped[:live_seqs], live_values),
                jnp.where(dead == live_seqs, skipped[live_seqs:], last),
            ],
            axis=0,
        )

    token_low = lax.optimization_barrier(pick(tokens))
    token_rows = token_low.astype(f32)
    down_grad = lax.optimization_barrier(pick(cotangent))

    hidden = (token_rows * rms_scale(token_rows) * gain_attn).astype(bf16)
    qkv_raw = dot(hidden, qkv_full, 1, 0)
    queries, kv_own = rope(qkv_raw, cosine, sine, rows, q_cols, k_cols)
    kv_own = kv_own.reshape(1, live_seqs, rows, 2 * k_cols)
    kv_near = kv_own
    for bits in [4 * bit for bit in reversed(far_bits)] + [2]:
        kv_near = jnp.concatenate([kv_near, flip(kv_near, bits)], axis=0)
    kv_other = flip(kv_near, 1)
    mixed_out, log_total = attend(
        queries, kv_near, kv_other, qpos, kpos, rows, local_kv, group
    )
    branch = tensor_total(dot(mixed_out, out_turned, 1, 1))
    middle = token_rows + branch

    hidden_mlp = (middle * rms_scale(middle) * gain_mlp).astype(bf16)
    gate_values, up_values, product = feed_forward(hidden_mlp, second, hidden_units)

    def side(a):
        keep, send = arrange(a, owners)
        return keep, flip(send, 1)

    def fold(kept, sent, bits):
        return kept.astype(f32) + flip(sent, bits).astype(f32)

    def fold_far(v, beside=None):
        for bit in far_bits:
            half = v.shape[0] // 2
            received = flip(v[half:], 4 * bit)
            if beside is not None:
                beside = beside[:half] + after(flip(beside[half:], 4 * bit), received)
            v = v[:half].astype(f32) + received.astype(f32)
            v = v if bit == far_bits[-1] else v.astype(bf16)
        return v, beside

    def send_pair(sent, *others):
        return flip(after(sent, *others) if others else sent, 2)

    def finish(a_side, b, b2, columns, received, beside=None):
        kept = side_product(a_side, 0, b, b2, columns, received)
        out, beside = fold_far(kept.reshape(groups, block, columns[1]), beside)
        out = out.reshape(block, columns[1])
        return out if beside is None else (out, beside)

    split_at = -(-hidden_units // 512) * 256
    hidden_cols = ((0, split_at), (split_at, hidden_units - split_at))
    down_side = side(down_grad)
    mlp_side = side(hidden_mlp)
    product2 = flip(product, 1)
    sent_down = [side_product(down_side, 1, product, product2, c) for c in hidden_cols]
    got_down = [send_pair(sent_down[0])]

    gate_grad, up_grad, hidden_partial = feed_forward_back(
        down_grad, gate_values, up_values, second, hidden_units, sent_down
    )
    gate_grad2, up_grad2 = flip(gate_grad, 1), flip(up_grad, 1)
    got_down.append(send_pair(sent_down[1], got_down[0]))
    hidden_partial = after(hidden_partial, got_down[0])
    hidden_theirs = tensor_flip(hidden_partial)
    sent_gate = [side_product(mlp_side, 1, gate_grad, gate_grad2, c) for c in hidden_cols]
    sent_up = [side_product(mlp_side, 1, up_grad, up_grad2, c) for c in hidden_cols]
    middle_grad, branch_grad, gain_mlp_rows = norm_back(
        hidden_partial, hidden_theirs, middle, gain_mlp, down_grad, rows,
        [*sent_gate, *sent_up, got_down[1]],
    )
    got_gate = [send_pair(sent_gate[0], got_down[1])]
    grad_down = [
        finish(down_side, product, product2, c, r)
        for c, r in zip(hidden_cols, got_down, strict=True)
    ]

    mixed_grad = dot(branch_grad, out_turned, 1, 0).astype(bf16)
    query_grad, dkv_near, dkv_other = attend_back(
        queries, kv_near, kv_other, qpos, kpos, log_total, mixed_grad,
        cosine, sine, rows, local_kv, group, [],
    )
    dkv = fold(dkv_near, dkv_other, 1).astype(bf16)
    got_dkv = flip(after(dkv[groups:], got_gate[0]), 2)
    dkv, _ = fold_far((dkv[:groups].astype(f32) + got_dkv.astype(f32)).astype(bf16))
    got_gate.append(send_pair(sent_gate[1], got_gate[0], got_dkv))
    grad_gate = [
        finish(mlp_side, gate_grad, gate_grad2, c, r)
        for c, r in zip(hidden_cols, got_gate, strict=True)
    ]
    got_up = [send_pair(sent_up[0], got_gate[1])]
    dkv = dkv.reshape(total, 2 * k_cols)
    key_grad, _ = rope(
        jnp.concatenate([dkv[:, :k_cols], dkv], axis=1), cosine, -sine, rows, k_cols, k_cols,
        [got_gate[1]],
    )
    qkv_grad = jnp.concatenate([query_grad, key_grad, dkv[:, k_cols:].astype(bf16)], axis=1)
    attn_side, qkv_grad2, all_cols = side(hidden), flip(qkv_grad, 1), (0, qkv_cols)
    sent_qkv = side_product(attn_side, 1, qkv_grad, qkv_grad2, all_cols, others=[got_up[0]])
    got_qkv = send_pair(sent_qkv)
    got_up.append(send_pair(sent_up[1], got_qkv))
    grad_up = [
        finish(mlp_side, up_grad, up_grad2, c, r)
        for c, r in zip(hidden_cols, got_up, strict=True)
    ]
    grad_qkv = finish(attn_side, qkv_grad, qkv_grad2, all_cols, got_qkv)
    attn_partial = dot(qkv_grad, qkv_full, 1, 1).astype(bf16)
    input_grad, _, gain_attn_rows = norm_back(
        attn_partial, tensor_flip(attn_partial), token_low, gain_attn, middle_grad, rows
    )
    input_grad = unpick(input_grad, cotangent.astype(f32))

    down_values = tensor_total(dot(after(product, query_grad), down_turned, 1, 1))
    result = unpick((middle + down_values).astype(bf16), tokens)

    gain_rows = jnp.concatenate([gain_attn_rows, gain_mlp_rows]).reshape(2, n_dp, block)
    gain_rows = jnp.take(gain_rows, owners, axis=1).transpose(1, 0, 2)
    gain_rows = gain_rows[: 2 * groups] + flip(gain_rows[2 * groups :], 1)
    out_side, mixed2, out_cols = side(branch_grad), flip(mixed_out, 1), (0, q_cols)
    sent_out = side_product(out_side, 1, mixed_out, mixed2, out_cols)
    got_gains = flip(after(gain_rows[groups:], got_qkv), 2)
    got_out = send_pair(sent_out, got_up[1])
    gain_rows = gain_rows[:groups] + after(got_gains, got_out)
    grad_out, gain_rows = finish(out_side, mixed_out, mixed2, out_cols, got_out, gain_rows)
    gain_own = gain_rows[0]

    return (
        result,
        input_grad,
        gain_own[0],
        grad_qkv[:, :q_cols],
        grad_qkv[:, q_cols : q_cols + k_cols],
        grad_qkv[:, q_cols + k_cols :],
        grad_out.T,
        gain_own[1],
        jnp.concatenate(grad_gate, axis=1),
        jnp.concatenate(grad_up, axis=1),
        jnp.concatenate(grad_down, axis=1).T,
    )


def solution(mesh):
    rows = P(None, "dp", None)
    split = P("dp", "tensor")
    turned = P("tensor", "dp")
    gain = P("dp")
    weights = (gain, split, split, split, turned, gain, split, split, turned)
    return jax.shard_map(
        functools.partial(local, mesh.shape["dp"]),
        mesh=mesh,
        in_specs=(rows, rows, P(), P(), *weights),
        out_specs=(rows, rows, *weights),
        check_vma=False,
    )
```

```python
import functools
import math

import jax
import jax.numpy as jnp
from jax import lax
from jax.experimental import pallas as pl
from jax.experimental.pallas import tpu as pltpu
from jax.sharding import PartitionSpec as P

HD = 128
EPSILON = 1e-05
NEGATIVE = -1e30
MIB = 1024 * 1024


def hint(microseconds):
    return pl.CostEstimate(
        flops=int(microseconds * 5e8), bytes_accessed=int(microseconds * 1.8e6), transcendentals=0
    )


FAR_FIRST = ("o",)
ORDER = (
    "fA", "fB", "PdA", "PdB", "F", "SdA", "H", "PgA", "SdB", "N", "SdA", "M", "A", "SgA", "SdB",
    "K", "PgB", "Sk", "V", "SdA", "SdA", "Sk", "SgA", "PuA", "SgB", "Sk", "SdB", "Sk", "R",
    "Po", "SgB", "Pq", "T", "SuA", "PuB", "So", "SgA", "Sq", "I", "SuA", "So", "SgB", "Sq",
    "SuA", "SuB", "So", "Sn", "Sq", "Sn", "SuB", "Sn", "SuB", "Sn",
)

bf16 = jnp.bfloat16
f32 = jnp.float32


def rms_scale(values):
    return lax.rsqrt(jnp.mean(values * values, axis=-1, keepdims=True) + EPSILON)


def dot(a, b, ca, cb):
    return lax.dot_general(a, b, (((ca,), (cb,)), ((), ())), preferred_element_type=f32)


def params(room=16 * MIB):
    return pltpu.CompilerParams(vmem_limit_bytes=min(room, 56 * MIB))


def turn(v, cosine, sine):
    return v * cosine + pltpu.roll(v, HD // 2, 1) * sine


def call(
    kernel, token, args, in_specs, outs, out_specs, name, takes, grid=(), scratch=(), others=(), aliases=None,
    room=16 * MIB,
):
    waits = [*([] if token is None else [token]), *others]
    unread = pl.BlockSpec(memory_space=pl.ANY)
    count = len(args)

    def body(*refs):
        rest = refs[count + len(waits) :]
        kernel(*refs[:count], *rest[: len(outs)], *rest[len(outs) + 1 :])

    return pl.pallas_call(
        body,
        grid=grid,
        in_specs=[*in_specs, *[unread] * len(waits)],
        out_specs=[*out_specs, unread],
        out_shape=[*outs, jax.ShapeDtypeStruct((8, 128), f32)],
        scratch_shapes=list(scratch),
        input_output_aliases=aliases or {},
        compiler_params=params(room),
        cost_estimate=hint(takes),
        name=name,
    )(*args, *waits)


def like(*shape, dtype=bf16):
    return jax.ShapeDtypeStruct(shape, dtype)


def rope_kernel(q_cols, k_cols, raw_ref, cos_ref, sin_ref, q_ref, kv_ref):
    cosine, sine = cos_ref[...], sin_ref[...]
    for c in range(0, q_cols, HD):
        q_ref[:, c : c + HD] = turn(raw_ref[:, c : c + HD], cosine, sine).astype(bf16)
    for c in range(0, k_cols, HD):
        v = raw_ref[:, q_cols + c : q_cols + c + HD]
        kv_ref[:, c : c + HD] = turn(v, cosine, sine).astype(bf16)
    kv_ref[:, k_cols:] = raw_ref[:, q_cols + k_cols :].astype(bf16)


def rope(raw, cosine, sine, rows, q_cols, k_cols, token=None):
    total, width = raw.shape
    table = pl.BlockSpec((rows, HD), lambda i: (0, 0))
    return call(
        functools.partial(rope_kernel, q_cols, k_cols),
        token,
        (raw, cosine, sine),
        [pl.BlockSpec((rows, width), lambda i: (i, 0)), table, table],
        [like(total, q_cols), like(total, 2 * k_cols)],
        [
            pl.BlockSpec((rows, q_cols), lambda i: (i, 0)),
            pl.BlockSpec((rows, 2 * k_cols), lambda i: (i, 0)),
        ],
        "rope",
        2,
        grid=(total // rows,),
    )


def heads_to_rows(block, kv, group):
    return jnp.concatenate(
        [block[:, (kv * group + g) * HD : (kv * group + g + 1) * HD] for g in range(group)], axis=0
    )


def keys_of(near_ref, far_ref, c):
    parts = [r[:, 0, :, c : c + HD].reshape(-1, HD) for r in (near_ref, far_ref)]
    return jnp.concatenate(parts, axis=0)


def attend_kernel(local_kv, group, q_ref, near_ref, far_ref, qpos_ref, kpos_ref, out_ref, log_ref):
    rows = q_ref.shape[0]
    allowed = kpos_ref[...] <= qpos_ref[...]
    for kv in range(local_kv):
        q = heads_to_rows(q_ref, kv, group)
        keys = keys_of(near_ref, far_ref, kv * HD)
        values = keys_of(near_ref, far_ref, (local_kv + kv) * HD)
        s = jnp.where(allowed, dot(q, keys, 1, 1) * (HD**-0.5), NEGATIVE)
        top = jnp.max(s, axis=-1, keepdims=True)
        e = jnp.exp(s - top)
        total = jnp.sum(e, axis=-1, keepdims=True)
        probs = (e * (1.0 / total)).astype(bf16)
        out = dot(probs, values, 1, 0)
        for g in range(group):
            c = (kv * group + g) * HD
            out_ref[:, c : c + HD] = out[g * rows : (g + 1) * rows].astype(bf16)
        log_ref[kv] = top + jnp.log(total)


def score_room(kpos, qpos):
    return 4 * MIB + 14 * 4 * kpos.size * qpos.size


def attend(q, near, far, qpos, kpos, rows, local_kv, group):
    total, width = q.shape
    seqs = total // rows
    blocks, _, _, kv_width = near.shape
    kv_spec = pl.BlockSpec((blocks, 1, rows, kv_width), lambda i: (0, i, 0, 0))
    return pl.pallas_call(
        functools.partial(attend_kernel, local_kv, group),
        grid=(seqs,),
        in_specs=[
            pl.BlockSpec((rows, width), lambda i: (i, 0)),
            kv_spec,
            kv_spec,
            pl.BlockSpec(qpos.shape, lambda i: (0, 0)),
            pl.BlockSpec(kpos.shape, lambda i: (0, 0)),
        ],
        out_specs=[
            pl.BlockSpec((rows, width), lambda i: (i, 0)),
            pl.BlockSpec((local_kv, group * rows, 1), lambda i: (i, 0, 0)),
        ],
        out_shape=[
            jax.ShapeDtypeStruct((total, width), bf16),
            jax.ShapeDtypeStruct((seqs * local_kv, group * rows, 1), f32),
        ],
        compiler_params=params(score_room(kpos, qpos)),
        cost_estimate=hint(9),
        name="attend",
    )(q, near, far, qpos, kpos)


def attend_back_kernel(
    local_kv, group, q_ref, near_ref, far_ref, qpos_ref, kpos_ref, log_ref, grad_ref, cos_ref, sin_ref,
    dq_ref, dnear_ref, dfar_ref,
):
    rows = q_ref.shape[0]
    half = near_ref.shape[0] * rows
    scale = HD**-0.5
    allowed = kpos_ref[...] <= qpos_ref[...]
    cosine, sine = cos_ref[...], sin_ref[...]
    for kv in range(local_kv):
        ck, cv = kv * HD, (local_kv + kv) * HD
        q = heads_to_rows(q_ref, kv, group)
        grad = heads_to_rows(grad_ref, kv, group)
        keys = keys_of(near_ref, far_ref, ck)
        values = keys_of(near_ref, far_ref, cv)
        s = jnp.where(allowed, dot(q, keys, 1, 1) * scale, NEGATIVE)
        probs = jnp.exp(s - log_ref[kv])
        prob_grad = dot(grad, values, 1, 1)
        both = probs * prob_grad
        delta = jnp.sum(both, axis=-1, keepdims=True)
        ds = (both - probs * delta).astype(bf16)
        dq = dot(ds, keys, 1, 0) * scale
        for g in range(group):
            c = (kv * group + g) * HD
            dq_ref[:, c : c + HD] = turn(dq[g * rows : (g + 1) * rows], cosine, -sine).astype(bf16)
        dk = (dot(ds, q, 0, 0) * scale).astype(bf16)
        dv = dot(probs.astype(bf16), grad, 0, 0).astype(bf16)
        for d, c in ((dk, ck), (dv, cv)):
            dnear_ref[:, 0, :, c : c + HD] = d[:half].reshape(-1, rows, HD)
            dfar_ref[:, 0, :, c : c + HD] = d[half:].reshape(-1, rows, HD)


def attend_back(
    q, near, far, qpos, kpos, log, grad, cosine, sine, rows, local_kv, group, token, others
):
    total, width = q.shape
    blocks, _, _, kv_width = near.shape
    kv_spec = pl.BlockSpec((blocks, 1, rows, kv_width), lambda i: (0, i, 0, 0))
    row_spec = pl.BlockSpec((rows, width), lambda i: (i, 0))
    table = pl.BlockSpec((rows, HD), lambda i: (0, 0))
    return call(
        functools.partial(attend_back_kernel, local_kv, group),
        token,
        (q, near, far, qpos, kpos, log, grad, cosine, sine),
        [
            row_spec,
            kv_spec,
            kv_spec,
            pl.BlockSpec(qpos.shape, lambda i: (0, 0)),
            pl.BlockSpec(kpos.shape, lambda i: (0, 0)),
            pl.BlockSpec((local_kv, group * rows, 1), lambda i: (i, 0, 0)),
            row_spec,
            table,
            table,
        ],
        [like(total, width), like(*near.shape), like(*far.shape)],
        [row_spec, kv_spec, kv_spec],
        "attend_back",
        13,
        grid=(total // rows,),
        others=others,
        room=score_room(kpos, qpos),
    )


def arrange_kernel(block, order_ref, a_ref, keep_ref, send_ref):
    half = order_ref.shape[0] // 2
    for j in range(half):
        for out_ref, at in ((keep_ref, j), (send_ref, half + j)):
            start = pl.multiple_of(order_ref[at] * block, block)
            out_ref[:, j * block : (j + 1) * block] = a_ref[:, pl.ds(start, block)]


def arrange(a, order):
    rows, width = a.shape
    count = order.shape[0]
    block = width // count
    if block % 128:
        moved = jnp.take(a.reshape(rows, count, block), order, axis=1).reshape(rows, width)
        return moved[:, : width // 2], moved[:, width // 2 :]
    out = jax.ShapeDtypeStruct((rows, width // 2), a.dtype)
    return pl.pallas_call(
        functools.partial(arrange_kernel, block),
        in_specs=[
            pl.BlockSpec(memory_space=pltpu.SMEM),
            pl.BlockSpec(memory_space=pltpu.VMEM),
        ],
        out_specs=[pl.BlockSpec(memory_space=pltpu.VMEM)] * 2,
        out_shape=[out, out],
        compiler_params=params(),
        cost_estimate=hint(1),
        name="arrange",
    )(order, a)


def forward_kernel(hidden_ref, gate_w_ref, up_w_ref, *refs):
    gate_ref, up_ref, product_ref = refs[-3:]
    hidden = hidden_ref[...]
    gate = dot(hidden, gate_w_ref[...], 1, 0)
    up = dot(hidden, up_w_ref[...], 1, 0)
    gate_ref[...] = gate
    up_ref[...] = up
    product_ref[...] = (gate * jax.nn.sigmoid(gate) * up).astype(bf16)


def feed_forward(hidden, weights, units, columns, before, token):
    rows, width = hidden.shape
    start, count = columns
    tile = math.gcd(math.gcd(start, count), math.gcd(units, 256))
    tiles, first = units // tile, start // tile
    column = pl.BlockSpec((rows, tile), lambda i: (0, first + i))
    return call(
        forward_kernel,
        token,
        (hidden, weights, weights, *before),
        [
            pl.BlockSpec((rows, width), lambda i: (0, 0)),
            pl.BlockSpec((width, tile), lambda i: (0, first + i)),
            pl.BlockSpec((width, tile), lambda i: (0, tiles + first + i)),
            *[pl.BlockSpec(memory_space=pl.ANY)] * len(before),
        ],
        [like(rows, units, dtype=f32), like(rows, units, dtype=f32), like(rows, count)],
        [column, column, pl.BlockSpec((rows, tile), lambda i: (0, i))],
        "feed_forward",
        17 * count / units,
        grid=(count // tile,),
        aliases={3: 0, 4: 1} if before else None,
    )


def backward_kernel(
    down_grad_ref, gate_ref, up_ref, gate_w_ref, up_w_ref, down_w_ref, grads_ref, partial_ref, sum_ref
):
    product_grad = dot(down_grad_ref[...], down_w_ref[...], 1, 0)
    gate, up = gate_ref[...], up_ref[...]
    sigmoid = jax.nn.sigmoid(gate)
    gate_grad = (product_grad * up * (sigmoid * (1.0 + gate * (1.0 - sigmoid)))).astype(bf16)
    up_grad = (product_grad * gate * sigmoid).astype(bf16)
    grads_ref[0] = gate_grad
    grads_ref[1] = up_grad
    term = dot(gate_grad, gate_w_ref[...], 1, 1) + dot(up_grad, up_w_ref[...], 1, 1)

    @pl.when(pl.program_id(0) == 0)
    def _():
        sum_ref[...] = term

    @pl.when(pl.program_id(0) != 0)
    def _():
        sum_ref[...] += term

    @pl.when(pl.program_id(0) == pl.num_programs(0) - 1)
    def _():
        partial_ref[...] = sum_ref[...].astype(bf16)


def feed_forward_back(down_grad, gate, up, weights, units, token):
    rows, width = down_grad.shape
    tile = math.gcd(units, 256)
    tiles = units // tile
    whole = pl.BlockSpec((rows, width), lambda i: (0, 0))
    column = pl.BlockSpec((rows, tile), lambda i: (0, i))
    return call(
        backward_kernel,
        token,
        (down_grad, gate, up, weights, weights, weights),
        [
            whole,
            column,
            column,
            pl.BlockSpec((width, tile), lambda i: (0, i)),
            pl.BlockSpec((width, tile), lambda i: (0, tiles + i)),
            pl.BlockSpec((width, tile), lambda i: (0, 2 * tiles + i)),
        ],
        [like(2, rows, units), like(rows, width)],
        [pl.BlockSpec((2, rows, tile), lambda i: (0, 0, i)), whole],
        "feed_forward_back",
        28,
        grid=(tiles,),
        scratch=[pltpu.VMEM((rows, width), f32)],
    )


def turned_kernel(a_ref, w_ref, out_ref):
    out_ref[...] = dot(a_ref[...], w_ref[...], 1, 1).astype(bf16)


def times_turned(a, weights, at, token):
    rows, depth = a.shape
    height = weights.shape[0]
    tile = math.gcd(height, 256)
    return call(
        turned_kernel,
        token,
        (a, weights),
        [
            pl.BlockSpec((rows, depth), lambda i: (0, 0)),
            pl.BlockSpec((tile, depth), lambda i: (i, at)),
        ],
        [like(rows, height)],
        [pl.BlockSpec((rows, tile), lambda i: (0, i))],
        "times_turned",
        9,
        grid=(height // tile,),
        room=48 * MIB,
    )


def product_kernel(blocks, a_ref, a2_ref, b_ref, b2_ref, *out_refs):
    for out_ref, chosen in zip(out_refs, blocks, strict=True):
        sides = []
        for ref in (a_ref, a2_ref):
            parts = [ref[:, start:end] for start, end in chosen]
            sides.append(parts[0] if len(parts) == 1 else jnp.concatenate(parts, axis=1))
        out = dot(sides[0], b_ref[...], 0, 0) + dot(sides[1], b2_ref[...], 0, 0)
        out_ref[...] = out.astype(bf16)


def side_products(side, b, b2, which, columns, blocks, token):
    a, a2 = side
    rows, width = a.shape
    start, count = columns
    tile = 768 if math.gcd(start, count) % 768 == 0 else math.gcd(start, count)
    first = start // tile
    whole = pl.BlockSpec((rows, width), lambda i: (0, 0))
    b_spec = pl.BlockSpec((None, rows, tile), lambda i: (which, 0, first + i))
    return call(
        functools.partial(product_kernel, blocks),
        token,
        (a, a2, b, b2),
        [whole, whole, b_spec, b_spec],
        [like(width // 2, count)] * 2,
        [pl.BlockSpec((width // 2, tile), lambda i: (0, i))] * 2,
        "side_products",
        6,
        grid=(count // tile,),
    )


def fold_kernel(kept_ref, received_ref, *out_refs):
    height = out_refs[0].shape[0]
    for i, out_ref in enumerate(out_refs):
        part = slice(i * height, (i + 1) * height)
        out = kept_ref[part].astype(f32) + received_ref[part].astype(f32)
        out_ref[...] = out.astype(out_ref.dtype)


def fold(kept, received, last, token):
    rows, width = kept.shape
    whole = pl.BlockSpec(memory_space=pltpu.VMEM)
    outs = [like(rows, width, dtype=f32)] if last else [like(rows // 2, width, dtype=kept.dtype)] * 2
    return call(
        fold_kernel, token, (kept, received), [whole] * 2, outs, [whole] * len(outs), "fold", 1.5,
        room=max(16 * MIB, 4 * MIB + 4 * kept.size * kept.dtype.itemsize),
    )


def hold_kernel(*refs):
    pass


def hold(v, token):
    anywhere = pl.BlockSpec(memory_space=pl.ANY)
    out = like(*v.shape, dtype=v.dtype)
    return call(
        hold_kernel, token, (v,), [anywhere], [out], [anywhere], "hold", 0.1, aliases={0: 0}
    )


def norm_back_kernel(
    mine_ref, theirs_ref, v_ref, gain_ref, base_ref, grad_ref, low_ref, gain_grad_ref
):
    hidden_grad = mine_ref[...].astype(f32) + theirs_ref[...].astype(f32)
    v = v_ref[...].astype(f32)
    scale = rms_scale(v)
    normed = v * scale
    gain_grad = jnp.sum(hidden_grad * normed, axis=0, keepdims=True)

    @pl.when(pl.program_id(0) == 0)
    def _():
        gain_grad_ref[...] = gain_grad

    @pl.when(pl.program_id(0) != 0)
    def _():
        gain_grad_ref[...] += gain_grad

    g = hidden_grad * gain_ref[...]
    out = base_ref[...].astype(f32) + scale * (
        g - normed * jnp.mean(g * normed, axis=-1, keepdims=True)
    )
    grad_ref[...] = out
    low_ref[...] = out.astype(bf16)


def norm_back(mine, theirs, v, gain, base, rows, token):
    total, width = mine.shape
    spec = pl.BlockSpec((rows, width), lambda i: (i, 0))
    row = pl.BlockSpec((1, width), lambda i: (0, 0))
    return call(
        norm_back_kernel,
        token,
        (mine, theirs, v, gain, base),
        [spec, spec, spec, row, spec],
        [like(total, width, dtype=f32), like(total, width), like(1, width, dtype=f32)],
        [spec, spec, row],
        "norm_back",
        6.5,
        grid=(total // rows,),
    )


def local(
    n_dp,
    tokens,
    cotangent,
    active,
    assignment,
    attention_gain,
    query_weight,
    key_weight,
    value_weight,
    out_weight,
    feedforward_gain,
    gate_weight,
    up_weight,
    down_weight,
):
    rows, width = tokens.shape[1:]
    live_seqs = tokens.shape[0] - 1
    total = live_seqs * rows
    block = width // n_dp
    groups = n_dp // 4
    q_cols, k_cols = query_weight.shape[1], key_weight.shape[1]
    hidden_units = gate_weight.shape[1]
    local_kv = k_cols // HD
    group = q_cols // k_cols
    me = lax.axis_index("dp").astype(jnp.int32)

    def flip(v, bits):
        return lax.ppermute(v, "dp", [(i, i ^ bits) for i in range(n_dp)])

    def tensor_flip(v):
        return lax.ppermute(v, "tensor", [(0, 1), (1, 0)])

    def tensor_total(partial_rows):
        mine = lax.optimization_barrier(partial_rows.astype(bf16))
        return mine.astype(f32) + tensor_flip(mine).astype(f32)

    far_bits = [1 << b for b in range(groups.bit_length() - 1)]
    fars = [0]
    for bit in reversed(far_bits):
        fars = fars + [far + bit for far in fars]
    near_places = [far * 4 + pair * 2 for pair in range(2) for far in fars]
    places = near_places + [place + 1 for place in near_places]
    owners = jnp.bitwise_xor(me, jnp.asarray(places, jnp.int32))

    positions = me * rows + jnp.arange(rows, dtype=jnp.int32)
    frequency = jnp.exp(
        -jnp.log(10000.0) * (2.0 * jnp.arange(HD // 2, dtype=f32) / HD)
    )
    angles = positions.astype(f32)[:, None] * frequency[None, :]
    cosine = jnp.concatenate([jnp.cos(angles)] * 2, axis=1)
    sine = jnp.concatenate([-jnp.sin(angles), jnp.sin(angles)], axis=1)
    qpos = jnp.tile(positions, group)[:, None]
    kpos = (owners[:, None] * rows + jnp.arange(rows, dtype=jnp.int32)[None, :]).reshape(1, -1)

    gains = jnp.stack([attention_gain, feedforward_gain], axis=1)
    gains = jnp.pad(gains, ((0, 0), (0, 126)))
    first = lax.all_gather(
        jnp.concatenate([query_weight, key_weight, value_weight, out_weight.T, gains], axis=1),
        "dp", axis=0, tiled=True,
    )
    second = lax.all_gather(
        jnp.concatenate([gate_weight, up_weight, down_weight.T], axis=1), "dp", axis=0, tiled=True
    )
    down_turned = second[:, 2 * hidden_units :]
    qkv_cols = q_cols + 2 * k_cols
    qkv_full = first[:, :qkv_cols]
    out_turned = first[:, qkv_cols : qkv_cols + q_cols]
    gain_attn_row = first[:, qkv_cols + q_cols].astype(f32)[None, :]
    gain_mlp = first[:, qkv_cols + q_cols + 1].astype(f32)[None, :]

    dead_slot = jnp.argmin(active.reshape(-1))
    dead = assignment[dead_slot]
    is_dead = (jnp.arange(live_seqs, dtype=jnp.int32) == dead)[:, None, None]

    def pick(v):
        return jnp.where(is_dead, v[live_seqs:], v[:live_seqs]).reshape(total, width)

    def unpick(live_values, skipped):
        live_values = live_values.reshape(live_seqs, rows, width)
        last = lax.dynamic_slice_in_dim(live_values, jnp.minimum(dead, live_seqs - 1), 1, 0)
        return jnp.concatenate(
            [
                jnp.where(is_dead, skipped[:live_seqs], live_values),
                jnp.where(dead == live_seqs, skipped[live_seqs:], last),
            ],
            axis=0,
        )

    token_low = lax.optimization_barrier(pick(tokens))
    token_rows = token_low.astype(f32)
    down_grad = lax.optimization_barrier(pick(cotangent))

    hidden = (token_rows * rms_scale(token_rows) * gain_attn_row).astype(bf16)
    qkv_raw = dot(hidden, qkv_full, 1, 0)
    queries, kv_own, _ = rope(qkv_raw, cosine, sine, rows, q_cols, k_cols)
    kv_own = kv_own.reshape(1, live_seqs, rows, 2 * k_cols)
    kv_near = kv_own
    for bits in [4 * bit for bit in reversed(far_bits)] + [2]:
        kv_near = jnp.concatenate([kv_near, flip(kv_near, bits)], axis=0)
    kv_other = flip(kv_near, 1)
    mixed_out, log_total = attend(
        queries, kv_near, kv_other, qpos, kpos, rows, local_kv, group
    )
    branch = tensor_total(dot(mixed_out, out_turned, 1, 1))
    middle = token_rows + branch

    hidden_mlp = (middle * rms_scale(middle) * gain_mlp).astype(bf16)
    def side(a):
        keep, send = arrange(a, owners)
        return keep, flip(send, 1)

    token = [None]

    def run(kernel, *args, **kwargs):
        *outs, token[0] = kernel(*args, **kwargs, token=token[0])
        return outs if len(outs) > 1 else outs[0]

    class Total:
        def __init__(self, kept, received, bits):
            self.kept, self.received, self.bits, self.out = kept, received, list(bits), None

        def step(self):
            if self.out is not None:
                return
            if not self.bits:
                self.out = run(fold, self.kept, self.received, True)
                return
            self.kept, sent = run(fold, self.kept, self.received, False)
            self.received = flip(sent, self.bits.pop(0))

        def end(self):
            while self.out is None:
                self.step()
            return self.out

    far_flips = [4 * bit for bit in far_bits]
    far_first = FAR_FIRST if block % 128 == 0 else ()

    def weight_total(name, *args):
        if name in far_first:
            places = [pair * groups + far for far in range(groups) for pair in range(2)]
            spans = [(place * block, (place + 1) * block) for place in places]
            blocks, bits = [spans[:groups], spans[groups:]], [*far_flips, 2]
        else:
            half = groups * block
            blocks, bits = [[(0, half)], [(half, 2 * half)]], [2, *far_flips]
        kept, sent = run(side_products, *args, blocks)
        return Total(kept, flip(sent, bits[0]), bits[1:])

    split_at = -(-hidden_units // 512) * 256
    columns = ((0, split_at), (split_at, hidden_units - split_at))
    down_side, mlp_side, attn_side = side(down_grad), side(hidden_mlp), side(hidden)
    mixed2 = flip(mixed_out, 1)
    arrived = [down_side[1], mlp_side[1], attn_side[1], mixed2]
    (token[0],) = call(hold_kernel, None, (), [], [], [], "hold", 0.1, others=arrived)

    totals, made = {}, {}
    kv_cols = 2 * k_cols
    chunks = {"A": columns[0], "B": columns[1]}

    def send_products(name):
        if name[0] == "d":
            product, product2 = made["product" + name[1]]
            args = (down_side, product[None], product2[None], 0, (0, product.shape[1]))
        elif name[0] in "gu":
            which = "gu".index(name[0])
            args = (mlp_side, made["grads"], made["grads2"], which, chunks[name[1]])
        elif name == "q":
            args = (attn_side, made["qkv_grad"][None], made["qkv_grad2"][None], 0, (0, qkv_cols))
        else:
            args = (made["out_side"], mixed_out[None], mixed2[None], 0, (0, q_cols))
        totals[name] = weight_total(name, *args)

    def feed(name):
        before = made.get("gate_up", ())
        *made["gate_up"], product = run(
            feed_forward, hidden_mlp, second, hidden_units, chunks[name], before
        )
        made["product" + name] = product, flip(product, 1)

    def feed_back():
        made["grads"], made["partial"] = run(
            feed_forward_back, down_grad, *made["gate_up"], second, hidden_units
        )

    def exchange():
        grads, partial = run(hold, made["grads"]), run(hold, made["partial"])
        made.update(grads=grads, grads2=flip(grads, 1), partial=partial, theirs=tensor_flip(partial))

    def middle_back():
        made["middle_grad"], made["branch_grad"], made["gain_mlp"] = run(
            norm_back, made["partial"], made["theirs"], middle, gain_mlp, down_grad, rows
        )

    def mixed_back():
        made["out_side"] = side(made["branch_grad"])
        made["mixed_grad"] = dot(made["branch_grad"], out_turned, 1, 0).astype(bf16)

    def attention_back():
        mixed_grad = made["mixed_grad"]
        made["query_grad"], made["near"], made["other"] = run(
            attend_back, queries, kv_near, kv_other, qpos, kpos, log_total, mixed_grad,
            cosine, sine, rows, local_kv, group, others=[made["out_side"][1]],
        )

    def keys_back():
        other = run(hold, made["other"])
        totals["k"] = Total(
            made["near"].reshape(-1, kv_cols), flip(other.reshape(-1, kv_cols), 1), [2, *far_flips]
        )

    def turn_back():
        dkv = totals["k"].end()
        key_grad, _ = run(
            rope, jnp.concatenate([dkv[:, :k_cols], dkv], axis=1), cosine, -sine, rows, k_cols, k_cols
        )
        qkv_grad = jnp.concatenate(
            [made["query_grad"], key_grad, dkv[:, k_cols:].astype(bf16)], axis=1
        )
        made.update(qkv_grad=qkv_grad, qkv_grad2=flip(qkv_grad, 1))

    def attention_partial():
        made["attn"] = run(times_turned, made["qkv_grad"], first, 0)
        made["attn_theirs"] = tensor_flip(made["attn"])

    def input_back():
        made["input_grad"], _, gain_attn = run(
            norm_back, made["attn"], made["attn_theirs"], token_low, gain_attn_row,
            made["middle_grad"], rows,
        )
        gains = jnp.concatenate([gain_attn, made["gain_mlp"]]).reshape(2, n_dp, block)
        gains = jnp.take(gains, owners, axis=1).transpose(1, 0, 2).reshape(n_dp, 2 * block)
        totals["n"] = Total(gains[: 2 * groups], flip(gains[2 * groups :], 1), [2, *far_flips])

    def down_value():
        product = jnp.concatenate([made["product" + name][0] for name in "AB"], axis=1)
        made["down"] = run(times_turned, product, second, 2)
        made["down_theirs"] = tensor_flip(made["down"])

    actions = {
        "F": feed_back, "H": exchange, "N": middle_back, "M": mixed_back, "A": attention_back, "K": keys_back,
        "R": turn_back, "T": attention_partial, "I": input_back, "V": down_value,
    }
    for entry in ORDER:
        if entry in actions:
            actions[entry]()
        elif entry[0] == "f":
            feed(entry[1])
        elif entry[0] == "P":
            send_products(entry[1:])
        else:
            totals[entry[1:]].step()
    finished = {name: v.end() for name, v in totals.items()}
    down_partial, down_theirs = made["down"], made["down_theirs"]
    input_grad, gains, grad_out, grad_qkv = (
        made["input_grad"], finished["n"], finished["o"], finished["q"],
    )
    grad_down, grad_gate, grad_up = [[finished[m + c] for c in "AB"] for m in "dgu"]
    down_values = down_partial.astype(f32) + down_theirs.astype(f32)
    result = unpick((middle + down_values).astype(bf16), tokens)
    input_grad = unpick(input_grad, cotangent.astype(f32))

    return (
        result,
        input_grad,
        gains[0, :block],
        grad_qkv[:, :q_cols],
        grad_qkv[:, q_cols : q_cols + k_cols],
        grad_qkv[:, q_cols + k_cols :],
        grad_out.T,
        gains[0, block:],
        jnp.concatenate(grad_gate, axis=1),
        jnp.concatenate(grad_up, axis=1),
        jnp.concatenate(grad_down, axis=1).T,
    )


def solution(mesh):
    rows = P(None, "dp", None)
    split = P("dp", "tensor")
    turned = P("tensor", "dp")
    gain = P("dp")
    weights = (gain, split, split, split, turned, gain, split, split, turned)
    return jax.shard_map(
        functools.partial(local, mesh.shape["dp"]),
        mesh=mesh,
        in_specs=(rows, rows, P(), P(), *weights),
        out_specs=(rows, rows, *weights),
        check_vma=False,
    )
```

```python
import functools
import math

import jax
import jax.numpy as jnp
from jax import lax
from jax.experimental import pallas as pl
from jax.experimental.pallas import tpu as pltpu
from jax.sharding import PartitionSpec as P

HD = 128
EPSILON = 1e-05
NEGATIVE = -1e30
MIB = 1024 * 1024


def hint(microseconds):
    return pl.CostEstimate(
        flops=int(microseconds * 5e8), bytes_accessed=int(microseconds * 1.8e6), transcendentals=0
    )


FAR_FIRST = ("o",)
ORDER = (
    "fA", "fB", "PdA", "PdB", "F", "SdA", "H", "PgA", "SdA", "SdB", "N", "M", "PgB", "A", "SdB",
    "SgA", "K", "Sk", "Sk", "V", "SdA", "PuA", "SgA", "SdA", "Sk", "SgB", "SdB", "Sk", "Po",
    "R", "SgB", "Pq", "T", "SuA", "PuB", "So", "SgA", "Sq", "I", "So", "SuA", "SuB", "Sq",
    "SgB", "SuA", "Sn", "SuB", "So", "Sq", "Sn", "Sn", "SuB", "Sn",
)

bf16 = jnp.bfloat16
f32 = jnp.float32


def rms_scale(values):
    return lax.rsqrt(jnp.mean(values * values, axis=-1, keepdims=True) + EPSILON)


def dot(a, b, ca, cb):
    return lax.dot_general(a, b, (((ca,), (cb,)), ((), ())), preferred_element_type=f32)


def params(room=20 * MIB):
    return pltpu.CompilerParams(vmem_limit_bytes=min(room, 56 * MIB))


def turn(v, cosine, sine):
    return v * cosine + pltpu.roll(v, HD // 2, 1) * sine


def call(
    kernel, token, args, in_specs, outs, out_specs, name, takes, grid=(), scratch=(), others=(), aliases=None,
    room=20 * MIB,
):
    waits = [*([] if token is None else [token]), *others]
    unread = pl.BlockSpec(memory_space=pl.ANY)
    count = len(args)

    def body(*refs):
        rest = refs[count + len(waits) :]
        kernel(*refs[:count], *rest[: len(outs)], *rest[len(outs) + 1 :])

    return pl.pallas_call(
        body,
        grid=grid,
        in_specs=[*in_specs, *[unread] * len(waits)],
        out_specs=[*out_specs, unread],
        out_shape=[*outs, jax.ShapeDtypeStruct((8, 128), f32)],
        scratch_shapes=list(scratch),
        input_output_aliases=aliases or {},
        compiler_params=params(room),
        cost_estimate=hint(takes),
        name=name,
    )(*args, *waits)


def like(*shape, dtype=bf16):
    return jax.ShapeDtypeStruct(shape, dtype)


def rope_kernel(q_cols, k_cols, raw_ref, cos_ref, sin_ref, q_ref, kv_ref):
    cosine, sine = cos_ref[...], sin_ref[...]
    for c in range(0, q_cols, HD):
        q_ref[:, c : c + HD] = turn(raw_ref[:, c : c + HD], cosine, sine).astype(bf16)
    for c in range(0, k_cols, HD):
        v = raw_ref[:, q_cols + c : q_cols + c + HD]
        kv_ref[:, c : c + HD] = turn(v, cosine, sine).astype(bf16)
    kv_ref[:, k_cols:] = raw_ref[:, q_cols + k_cols :].astype(bf16)


def rope(raw, cosine, sine, rows, q_cols, k_cols, token=None):
    total, width = raw.shape
    table = pl.BlockSpec((rows, HD), lambda i: (0, 0))
    return call(
        functools.partial(rope_kernel, q_cols, k_cols),
        token,
        (raw, cosine, sine),
        [pl.BlockSpec((rows, width), lambda i: (i, 0)), table, table],
        [like(total, q_cols), like(total, 2 * k_cols)],
        [
            pl.BlockSpec((rows, q_cols), lambda i: (i, 0)),
            pl.BlockSpec((rows, 2 * k_cols), lambda i: (i, 0)),
        ],
        "rope",
        2,
        grid=(total // rows,),
    )


def heads_to_rows(block, kv, group):
    return jnp.concatenate(
        [block[:, (kv * group + g) * HD : (kv * group + g + 1) * HD] for g in range(group)], axis=0
    )


def keys_of(near_ref, far_ref, c):
    parts = [r[:, 0, :, c : c + HD].reshape(-1, HD) for r in (near_ref, far_ref)]
    return jnp.concatenate(parts, axis=0)


def attend_kernel(local_kv, group, q_ref, near_ref, far_ref, qpos_ref, kpos_ref, out_ref, log_ref):
    rows = q_ref.shape[0]
    allowed = kpos_ref[...] <= qpos_ref[...]
    for kv in range(local_kv):
        q = heads_to_rows(q_ref, kv, group)
        keys = keys_of(near_ref, far_ref, kv * HD)
        values = keys_of(near_ref, far_ref, (local_kv + kv) * HD)
        s = jnp.where(allowed, dot(q, keys, 1, 1) * (HD**-0.5), NEGATIVE)
        top = jnp.max(s, axis=-1, keepdims=True)
        e = jnp.exp(s - top)
        total = jnp.sum(e, axis=-1, keepdims=True)
        probs = (e * (1.0 / total)).astype(bf16)
        out = dot(probs, values, 1, 0)
        for g in range(group):
            c = (kv * group + g) * HD
            out_ref[:, c : c + HD] = out[g * rows : (g + 1) * rows].astype(bf16)
        log_ref[kv] = top + jnp.log(total)


def score_room(kpos, qpos):
    return 4 * MIB + 14 * 4 * kpos.size * qpos.size


def attend(q, near, far, qpos, kpos, rows, local_kv, group):
    total, width = q.shape
    seqs = total // rows
    blocks, _, _, kv_width = near.shape
    kv_spec = pl.BlockSpec((blocks, 1, rows, kv_width), lambda i: (0, i, 0, 0))
    return pl.pallas_call(
        functools.partial(attend_kernel, local_kv, group),
        grid=(seqs,),
        in_specs=[
            pl.BlockSpec((rows, width), lambda i: (i, 0)),
            kv_spec,
            kv_spec,
            pl.BlockSpec(qpos.shape, lambda i: (0, 0)),
            pl.BlockSpec(kpos.shape, lambda i: (0, 0)),
        ],
        out_specs=[
            pl.BlockSpec((rows, width), lambda i: (i, 0)),
            pl.BlockSpec((local_kv, group * rows, 1), lambda i: (i, 0, 0)),
        ],
        out_shape=[
            jax.ShapeDtypeStruct((total, width), bf16),
            jax.ShapeDtypeStruct((seqs * local_kv, group * rows, 1), f32),
        ],
        compiler_params=params(score_room(kpos, qpos)),
        cost_estimate=hint(9),
        name="attend",
    )(q, near, far, qpos, kpos)


def attend_back_kernel(
    local_kv, group, q_ref, near_ref, far_ref, qpos_ref, kpos_ref, log_ref, grad_ref, cos_ref, sin_ref,
    dq_ref, dnear_ref, dfar_ref,
):
    rows = q_ref.shape[0]
    half = near_ref.shape[0] * rows
    scale = HD**-0.5
    allowed = kpos_ref[...] <= qpos_ref[...]
    cosine, sine = cos_ref[...], sin_ref[...]
    for kv in range(local_kv):
        ck, cv = kv * HD, (local_kv + kv) * HD
        q = heads_to_rows(q_ref, kv, group)
        grad = heads_to_rows(grad_ref, kv, group)
        keys = keys_of(near_ref, far_ref, ck)
        values = keys_of(near_ref, far_ref, cv)
        s = jnp.where(allowed, dot(q, keys, 1, 1) * scale, NEGATIVE)
        probs = jnp.exp(s - log_ref[kv])
        prob_grad = dot(grad, values, 1, 1)
        both = probs * prob_grad
        delta = jnp.sum(both, axis=-1, keepdims=True)
        ds = (both - probs * delta).astype(bf16)
        dq = dot(ds, keys, 1, 0) * scale
        for g in range(group):
            c = (kv * group + g) * HD
            dq_ref[:, c : c + HD] = turn(dq[g * rows : (g + 1) * rows], cosine, -sine).astype(bf16)
        dk = (dot(ds, q, 0, 0) * scale).astype(bf16)
        dv = dot(probs.astype(bf16), grad, 0, 0).astype(bf16)
        for d, c in ((dk, ck), (dv, cv)):
            dnear_ref[:, 0, :, c : c + HD] = d[:half].reshape(-1, rows, HD)
            dfar_ref[:, 0, :, c : c + HD] = d[half:].reshape(-1, rows, HD)


def attend_back(
    q, near, far, qpos, kpos, log, grad, cosine, sine, rows, local_kv, group, token, others
):
    total, width = q.shape
    blocks, _, _, kv_width = near.shape
    kv_spec = pl.BlockSpec((blocks, 1, rows, kv_width), lambda i: (0, i, 0, 0))
    row_spec = pl.BlockSpec((rows, width), lambda i: (i, 0))
    table = pl.BlockSpec((rows, HD), lambda i: (0, 0))
    return call(
        functools.partial(attend_back_kernel, local_kv, group),
        token,
        (q, near, far, qpos, kpos, log, grad, cosine, sine),
        [
            row_spec,
            kv_spec,
            kv_spec,
            pl.BlockSpec(qpos.shape, lambda i: (0, 0)),
            pl.BlockSpec(kpos.shape, lambda i: (0, 0)),
            pl.BlockSpec((local_kv, group * rows, 1), lambda i: (i, 0, 0)),
            row_spec,
            table,
            table,
        ],
        [like(total, width), like(*near.shape), like(*far.shape)],
        [row_spec, kv_spec, kv_spec],
        "attend_back",
        13,
        grid=(total // rows,),
        others=others,
        room=score_room(kpos, qpos),
    )


def arrange_kernel(block, order_ref, a_ref, keep_ref, send_ref):
    half = order_ref.shape[0] // 2
    for j in range(half):
        for out_ref, at in ((keep_ref, j), (send_ref, half + j)):
            start = pl.multiple_of(order_ref[at] * block, block)
            out_ref[:, j * block : (j + 1) * block] = a_ref[:, pl.ds(start, block)]


def arrange(a, order):
    rows, width = a.shape
    count = order.shape[0]
    block = width // count
    if block % 128:
        moved = jnp.take(a.reshape(rows, count, block), order, axis=1).reshape(rows, width)
        return moved[:, : width // 2], moved[:, width // 2 :]
    out = jax.ShapeDtypeStruct((rows, width // 2), a.dtype)
    return pl.pallas_call(
        functools.partial(arrange_kernel, block),
        in_specs=[
            pl.BlockSpec(memory_space=pltpu.SMEM),
            pl.BlockSpec(memory_space=pltpu.VMEM),
        ],
        out_specs=[pl.BlockSpec(memory_space=pltpu.VMEM)] * 2,
        out_shape=[out, out],
        compiler_params=params(),
        cost_estimate=hint(1),
        name="arrange",
    )(order, a)


def forward_kernel(hidden_ref, gate_w_ref, up_w_ref, *refs):
    gate_ref, up_ref, product_ref = refs[-3:]
    hidden = hidden_ref[...]
    gate = dot(hidden, gate_w_ref[...], 1, 0)
    up = dot(hidden, up_w_ref[...], 1, 0)
    gate_ref[...] = gate
    up_ref[...] = up
    product_ref[...] = (gate * jax.nn.sigmoid(gate) * up).astype(bf16)


def feed_forward(hidden, weights, units, columns, before, token):
    rows, width = hidden.shape
    start, count = columns
    tile = math.gcd(math.gcd(start, count), math.gcd(units, 256))
    tiles, first = units // tile, start // tile
    column = pl.BlockSpec((rows, tile), lambda i: (0, first + i))
    return call(
        forward_kernel,
        token,
        (hidden, weights, weights, *before),
        [
            pl.BlockSpec((rows, width), lambda i: (0, 0)),
            pl.BlockSpec((width, tile), lambda i: (0, first + i)),
            pl.BlockSpec((width, tile), lambda i: (0, tiles + first + i)),
            *[pl.BlockSpec(memory_space=pl.ANY)] * len(before),
        ],
        [like(rows, units, dtype=f32), like(rows, units, dtype=f32), like(rows, count)],
        [column, column, pl.BlockSpec((rows, tile), lambda i: (0, i))],
        "feed_forward",
        17 * count / units,
        grid=(count // tile,),
        aliases={3: 0, 4: 1} if before else None,
    )


def backward_kernel(
    down_grad_ref, gate_ref, up_ref, gate_w_ref, up_w_ref, down_w_ref, grads_ref, partial_ref, sum_ref
):
    product_grad = dot(down_grad_ref[...], down_w_ref[...], 1, 0)
    gate, up = gate_ref[...], up_ref[...]
    sigmoid = jax.nn.sigmoid(gate)
    gate_grad = (product_grad * up * (sigmoid * (1.0 + gate * (1.0 - sigmoid)))).astype(bf16)
    up_grad = (product_grad * gate * sigmoid).astype(bf16)
    grads_ref[0] = gate_grad
    grads_ref[1] = up_grad
    term = dot(gate_grad, gate_w_ref[...], 1, 1) + dot(up_grad, up_w_ref[...], 1, 1)

    @pl.when(pl.program_id(0) == 0)
    def _():
        sum_ref[...] = term

    @pl.when(pl.program_id(0) != 0)
    def _():
        sum_ref[...] += term

    @pl.when(pl.program_id(0) == pl.num_programs(0) - 1)
    def _():
        partial_ref[...] = sum_ref[...].astype(bf16)


def feed_forward_back(down_grad, gate, up, weights, units, token):
    rows, width = down_grad.shape
    tile = math.gcd(units, 256)
    tiles = units // tile
    whole = pl.BlockSpec((rows, width), lambda i: (0, 0))
    column = pl.BlockSpec((rows, tile), lambda i: (0, i))
    return call(
        backward_kernel,
        token,
        (down_grad, gate, up, weights, weights, weights),
        [
            whole,
            column,
            column,
            pl.BlockSpec((width, tile), lambda i: (0, i)),
            pl.BlockSpec((width, tile), lambda i: (0, tiles + i)),
            pl.BlockSpec((width, tile), lambda i: (0, 2 * tiles + i)),
        ],
        [like(2, rows, units), like(rows, width)],
        [pl.BlockSpec((2, rows, tile), lambda i: (0, 0, i)), whole],
        "feed_forward_back",
        28,
        grid=(tiles,),
        scratch=[pltpu.VMEM((rows, width), f32)],
    )


def turned_kernel(a_ref, w_ref, out_ref):
    out_ref[...] = dot(a_ref[...], w_ref[...], 1, 1).astype(bf16)


def times_turned(a, weights, at, token):
    rows, depth = a.shape
    height = weights.shape[0]
    tile = math.gcd(height, 256)
    return call(
        turned_kernel,
        token,
        (a, weights),
        [
            pl.BlockSpec((rows, depth), lambda i: (0, 0)),
            pl.BlockSpec((tile, depth), lambda i: (i, at)),
        ],
        [like(rows, height)],
        [pl.BlockSpec((rows, tile), lambda i: (0, i))],
        "times_turned",
        9,
        grid=(height // tile,),
        room=48 * MIB,
    )


def product_kernel(blocks, a_ref, a2_ref, b_ref, b2_ref, *out_refs):
    for out_ref, chosen in zip(out_refs, blocks, strict=True):
        sides = []
        for ref in (a_ref, a2_ref):
            parts = [ref[:, start:end] for start, end in chosen]
            sides.append(parts[0] if len(parts) == 1 else jnp.concatenate(parts, axis=1))
        out = dot(sides[0], b_ref[...], 0, 0) + dot(sides[1], b2_ref[...], 0, 0)
        out_ref[...] = out.astype(bf16)


def side_products(side, b, b2, which, columns, blocks, token):
    a, a2 = side
    rows, width = a.shape
    start, count = columns
    tile = 768 if math.gcd(start, count) % 768 == 0 else math.gcd(start, count)
    first = start // tile
    whole = pl.BlockSpec((rows, width), lambda i: (0, 0))
    b_spec = pl.BlockSpec((None, rows, tile), lambda i: (which, 0, first + i))
    return call(
        functools.partial(product_kernel, blocks),
        token,
        (a, a2, b, b2),
        [whole, whole, b_spec, b_spec],
        [like(width // 2, count)] * 2,
        [pl.BlockSpec((width // 2, tile), lambda i: (0, i))] * 2,
        "side_products",
        6,
        grid=(count // tile,),
    )


def fold_kernel(kept_ref, received_ref, *out_refs):
    height = out_refs[0].shape[0]
    for i, out_ref in enumerate(out_refs):
        part = slice(i * height, (i + 1) * height)
        out = kept_ref[part].astype(f32) + received_ref[part].astype(f32)
        out_ref[...] = out.astype(out_ref.dtype)


def fold(kept, received, last, token):
    rows, width = kept.shape
    whole = pl.BlockSpec(memory_space=pltpu.VMEM)
    outs = [like(rows, width, dtype=f32)] if last else [like(rows // 2, width, dtype=kept.dtype)] * 2
    return call(
        fold_kernel, token, (kept, received), [whole] * 2, outs, [whole] * len(outs), "fold", 1.5,
        room=max(20 * MIB, 4 * MIB + 4 * kept.size * kept.dtype.itemsize),
    )


def hold_kernel(*refs):
    pass


def hold(v, token):
    anywhere = pl.BlockSpec(memory_space=pl.ANY)
    out = like(*v.shape, dtype=v.dtype)
    return call(
        hold_kernel, token, (v,), [anywhere], [out], [anywhere], "hold", 0.1, aliases={0: 0}
    )


def norm_back_kernel(
    mine_ref, theirs_ref, v_ref, gain_ref, base_ref, grad_ref, low_ref, gain_grad_ref
):
    hidden_grad = mine_ref[...].astype(f32) + theirs_ref[...].astype(f32)
    v = v_ref[...].astype(f32)
    scale = rms_scale(v)
    normed = v * scale
    gain_grad = jnp.sum(hidden_grad * normed, axis=0, keepdims=True)

    @pl.when(pl.program_id(0) == 0)
    def _():
        gain_grad_ref[...] = gain_grad

    @pl.when(pl.program_id(0) != 0)
    def _():
        gain_grad_ref[...] += gain_grad

    g = hidden_grad * gain_ref[...]
    out = base_ref[...].astype(f32) + scale * (
        g - normed * jnp.mean(g * normed, axis=-1, keepdims=True)
    )
    grad_ref[...] = out
    low_ref[...] = out.astype(bf16)


def norm_back(mine, theirs, v, gain, base, rows, token):
    total, width = mine.shape
    spec = pl.BlockSpec((rows, width), lambda i: (i, 0))
    row = pl.BlockSpec((1, width), lambda i: (0, 0))
    return call(
        norm_back_kernel,
        token,
        (mine, theirs, v, gain, base),
        [spec, spec, spec, row, spec],
        [like(total, width, dtype=f32), like(total, width), like(1, width, dtype=f32)],
        [spec, spec, row],
        "norm_back",
        6.5,
        grid=(total // rows,),
    )


def local(
    n_dp,
    tokens,
    cotangent,
    active,
    assignment,
    attention_gain,
    query_weight,
    key_weight,
    value_weight,
    out_weight,
    feedforward_gain,
    gate_weight,
    up_weight,
    down_weight,
):
    rows, width = tokens.shape[1:]
    live_seqs = tokens.shape[0] - 1
    total = live_seqs * rows
    block = width // n_dp
    groups = n_dp // 4
    q_cols, k_cols = query_weight.shape[1], key_weight.shape[1]
    hidden_units = gate_weight.shape[1]
    local_kv = k_cols // HD
    group = q_cols // k_cols
    me = lax.axis_index("dp").astype(jnp.int32)

    def flip(v, bits):
        return lax.ppermute(v, "dp", [(i, i ^ bits) for i in range(n_dp)])

    def tensor_flip(v):
        return lax.ppermute(v, "tensor", [(0, 1), (1, 0)])

    def tensor_total(partial_rows):
        mine = lax.optimization_barrier(partial_rows.astype(bf16))
        return mine.astype(f32) + tensor_flip(mine).astype(f32)

    far_bits = [1 << b for b in range(groups.bit_length() - 1)]
    fars = [0]
    for bit in reversed(far_bits):
        fars = fars + [far + bit for far in fars]
    near_places = [far * 4 + pair * 2 for pair in range(2) for far in fars]
    places = near_places + [place + 1 for place in near_places]
    owners = jnp.bitwise_xor(me, jnp.asarray(places, jnp.int32))

    positions = me * rows + jnp.arange(rows, dtype=jnp.int32)
    frequency = jnp.exp(
        -jnp.log(10000.0) * (2.0 * jnp.arange(HD // 2, dtype=f32) / HD)
    )
    angles = positions.astype(f32)[:, None] * frequency[None, :]
    cosine = jnp.concatenate([jnp.cos(angles)] * 2, axis=1)
    sine = jnp.concatenate([-jnp.sin(angles), jnp.sin(angles)], axis=1)
    qpos = jnp.tile(positions, group)[:, None]
    kpos = (owners[:, None] * rows + jnp.arange(rows, dtype=jnp.int32)[None, :]).reshape(1, -1)

    gains = jnp.stack([attention_gain, feedforward_gain], axis=1)
    gains = jnp.pad(gains, ((0, 0), (0, 126)))
    first = lax.all_gather(
        jnp.concatenate([query_weight, key_weight, value_weight, out_weight.T, gains], axis=1),
        "dp", axis=0, tiled=True,
    )
    second = lax.all_gather(
        jnp.concatenate([gate_weight, up_weight, down_weight.T], axis=1), "dp", axis=0, tiled=True
    )
    down_turned = second[:, 2 * hidden_units :]
    qkv_cols = q_cols + 2 * k_cols
    qkv_full = first[:, :qkv_cols]
    out_turned = first[:, qkv_cols : qkv_cols + q_cols]
    gain_attn_row = first[:, qkv_cols + q_cols].astype(f32)[None, :]
    gain_mlp = first[:, qkv_cols + q_cols + 1].astype(f32)[None, :]

    dead_slot = jnp.argmin(active.reshape(-1))
    dead = assignment[dead_slot]
    is_dead = (jnp.arange(live_seqs, dtype=jnp.int32) == dead)[:, None, None]

    def pick(v):
        return jnp.where(is_dead, v[live_seqs:], v[:live_seqs]).reshape(total, width)

    def unpick(live_values, skipped):
        live_values = live_values.reshape(live_seqs, rows, width)
        last = lax.dynamic_slice_in_dim(live_values, jnp.minimum(dead, live_seqs - 1), 1, 0)
        return jnp.concatenate(
            [
                jnp.where(is_dead, skipped[:live_seqs], live_values),
                jnp.where(dead == live_seqs, skipped[live_seqs:], last),
            ],
            axis=0,
        )

    token_low = lax.optimization_barrier(pick(tokens))
    token_rows = token_low.astype(f32)
    down_grad = lax.optimization_barrier(pick(cotangent))

    hidden = (token_rows * rms_scale(token_rows) * gain_attn_row).astype(bf16)
    qkv_raw = dot(hidden, qkv_full, 1, 0)
    queries, kv_own, _ = rope(qkv_raw, cosine, sine, rows, q_cols, k_cols)
    kv_own = kv_own.reshape(1, live_seqs, rows, 2 * k_cols)
    kv_near = kv_own
    for bits in [4 * bit for bit in reversed(far_bits)] + [2]:
        kv_near = jnp.concatenate([kv_near, flip(kv_near, bits)], axis=0)
    kv_other = flip(kv_near, 1)
    mixed_out, log_total = attend(
        queries, kv_near, kv_other, qpos, kpos, rows, local_kv, group
    )
    branch = tensor_total(dot(mixed_out, out_turned, 1, 1))
    middle = token_rows + branch

    hidden_mlp = (middle * rms_scale(middle) * gain_mlp).astype(bf16)
    def side(a):
        keep, send = arrange(a, owners)
        return keep, flip(send, 1)

    token = [None]

    def run(kernel, *args, **kwargs):
        *outs, token[0] = kernel(*args, **kwargs, token=token[0])
        return outs if len(outs) > 1 else outs[0]

    class Total:
        def __init__(self, kept, received, bits):
            self.kept, self.received, self.bits, self.out = kept, received, list(bits), None

        def step(self):
            if self.out is not None:
                return
            if not self.bits:
                self.out = run(fold, self.kept, self.received, True)
                return
            self.kept, sent = run(fold, self.kept, self.received, False)
            self.received = flip(sent, self.bits.pop(0))

        def end(self):
            while self.out is None:
                self.step()
            return self.out

    far_flips = [4 * bit for bit in far_bits]
    far_first = FAR_FIRST if block % 128 == 0 else ()

    def weight_total(name, *args):
        if name in far_first:
            places = [pair * groups + far for far in range(groups) for pair in range(2)]
            spans = [(place * block, (place + 1) * block) for place in places]
            blocks, bits = [spans[:groups], spans[groups:]], [*far_flips, 2]
        else:
            half = groups * block
            blocks, bits = [[(0, half)], [(half, 2 * half)]], [2, *far_flips]
        kept, sent = run(side_products, *args, blocks)
        return Total(kept, flip(sent, bits[0]), bits[1:])

    split_at = -(-hidden_units // 512) * 256
    columns = ((0, split_at), (split_at, hidden_units - split_at))
    down_side, mlp_side, attn_side = side(down_grad), side(hidden_mlp), side(hidden)
    mixed2 = flip(mixed_out, 1)
    arrived = [down_side[1], mlp_side[1], attn_side[1], mixed2]
    (token[0],) = call(hold_kernel, None, (), [], [], [], "hold", 0.1, others=arrived)

    totals, made = {}, {}
    kv_cols = 2 * k_cols
    chunks = {"A": columns[0], "B": columns[1]}

    def send_products(name):
        if name[0] == "d":
            product, product2 = made["product" + name[1]]
            args = (down_side, product[None], product2[None], 0, (0, product.shape[1]))
        elif name[0] in "gu":
            which = "gu".index(name[0])
            args = (mlp_side, made["grads"], made["grads2"], which, chunks[name[1]])
        elif name == "q":
            args = (attn_side, made["qkv_grad"][None], made["qkv_grad2"][None], 0, (0, qkv_cols))
        else:
            args = (made["out_side"], mixed_out[None], mixed2[None], 0, (0, q_cols))
        totals[name] = weight_total(name, *args)

    def feed(name):
        before = made.get("gate_up", ())
        *made["gate_up"], product = run(
            feed_forward, hidden_mlp, second, hidden_units, chunks[name], before
        )
        made["product" + name] = product, flip(product, 1)

    def feed_back():
        made["grads"], made["partial"] = run(
            feed_forward_back, down_grad, *made["gate_up"], second, hidden_units
        )

    def exchange():
        grads, partial = run(hold, made["grads"]), run(hold, made["partial"])
        made.update(grads=grads, grads2=flip(grads, 1), partial=partial, theirs=tensor_flip(partial))

    def middle_back():
        made["middle_grad"], made["branch_grad"], made["gain_mlp"] = run(
            norm_back, made["partial"], made["theirs"], middle, gain_mlp, down_grad, rows
        )

    def mixed_back():
        made["out_side"] = side(made["branch_grad"])
        made["mixed_grad"] = dot(made["branch_grad"], out_turned, 1, 0).astype(bf16)

    def attention_back():
        mixed_grad = made["mixed_grad"]
        made["query_grad"], made["near"], made["other"] = run(
            attend_back, queries, kv_near, kv_other, qpos, kpos, log_total, mixed_grad,
            cosine, sine, rows, local_kv, group, others=[made["out_side"][1]],
        )

    def keys_back():
        other = run(hold, made["other"])
        totals["k"] = Total(
            made["near"].reshape(-1, kv_cols), flip(other.reshape(-1, kv_cols), 1), [2, *far_flips]
        )

    def turn_back():
        dkv = totals["k"].end()
        key_grad, _ = run(
            rope, jnp.concatenate([dkv[:, :k_cols], dkv], axis=1), cosine, -sine, rows, k_cols, k_cols
        )
        qkv_grad = jnp.concatenate(
            [made["query_grad"], key_grad, dkv[:, k_cols:].astype(bf16)], axis=1
        )
        made.update(qkv_grad=qkv_grad, qkv_grad2=flip(qkv_grad, 1))

    def attention_partial():
        made["attn"] = run(times_turned, made["qkv_grad"], first, 0)
        made["attn_theirs"] = tensor_flip(made["attn"])

    def input_back():
        made["input_grad"], _, gain_attn = run(
            norm_back, made["attn"], made["attn_theirs"], token_low, gain_attn_row,
            made["middle_grad"], rows,
        )
        gains = jnp.concatenate([gain_attn, made["gain_mlp"]]).reshape(2, n_dp, block)
        gains = jnp.take(gains, owners, axis=1).transpose(1, 0, 2).reshape(n_dp, 2 * block)
        totals["n"] = Total(gains[: 2 * groups], flip(gains[2 * groups :], 1), [2, *far_flips])

    def down_value():
        product = jnp.concatenate([made["product" + name][0] for name in "AB"], axis=1)
        made["down"] = run(times_turned, product, second, 2)
        made["down_theirs"] = tensor_flip(made["down"])

    actions = {
        "F": feed_back, "H": exchange, "N": middle_back, "M": mixed_back, "A": attention_back, "K": keys_back,
        "R": turn_back, "T": attention_partial, "I": input_back, "V": down_value,
    }
    for entry in ORDER:
        if entry in actions:
            actions[entry]()
        elif entry[0] == "f":
            feed(entry[1])
        elif entry[0] == "P":
            send_products(entry[1:])
        else:
            totals[entry[1:]].step()
    finished = {name: v.end() for name, v in totals.items()}
    down_partial, down_theirs = made["down"], made["down_theirs"]
    input_grad, gains, grad_out, grad_qkv = (
        made["input_grad"], finished["n"], finished["o"], finished["q"],
    )
    grad_down, grad_gate, grad_up = [[finished[m + c] for c in "AB"] for m in "dgu"]
    down_values = down_partial.astype(f32) + down_theirs.astype(f32)
    result = unpick((middle + down_values).astype(bf16), tokens)
    input_grad = unpick(input_grad, cotangent.astype(f32))

    return (
        result,
        input_grad,
        gains[0, :block],
        grad_qkv[:, :q_cols],
        grad_qkv[:, q_cols : q_cols + k_cols],
        grad_qkv[:, q_cols + k_cols :],
        grad_out.T,
        gains[0, block:],
        jnp.concatenate(grad_gate, axis=1),
        jnp.concatenate(grad_up, axis=1),
        jnp.concatenate(grad_down, axis=1).T,
    )


def solution(mesh):
    rows = P(None, "dp", None)
    split = P("dp", "tensor")
    turned = P("tensor", "dp")
    gain = P("dp")
    weights = (gain, split, split, split, turned, gain, split, split, turned)
    return jax.shard_map(
        functools.partial(local, mesh.shape["dp"]),
        mesh=mesh,
        in_specs=(rows, rows, P(), P(), *weights),
        out_specs=(rows, rows, *weights),
        check_vma=False,
    )
```

```python
import functools
import math

import jax
import jax.numpy as jnp
from jax import lax
from jax.experimental import pallas as pl
from jax.experimental.pallas import tpu as pltpu
from jax.sharding import PartitionSpec as P

HD = 128
EPSILON = 1e-05
NEGATIVE = -1e30
MIB = 1024 * 1024


def hint(microseconds):
    return pl.CostEstimate(
        flops=int(microseconds * 5e8), bytes_accessed=int(microseconds * 1.8e6), transcendentals=0
    )


FAR_FIRST = ("o",)
ORDER = (
    "fA", "fB", "PdA", "PdB", "F", "SdA", "H", "PgA", "SdB", "N", "SdA", "M", "A", "SgA", "SdB",
    "K", "PgB", "Sk", "V", "SdA", "SdA", "Sk", "SgA", "PuA", "SgB", "Sk", "SdB", "Sk", "R",
    "Po", "SgB", "Pq", "T", "SuA", "PuB", "So", "SgA", "Sq", "I", "SuA", "So", "SgB", "Sq",
    "SuA", "SuB", "So", "Sn", "Sq", "Sn", "SuB", "Sn", "SuB", "Sn",
)

bf16 = jnp.bfloat16
f32 = jnp.float32


def rms_scale(values):
    return lax.rsqrt(jnp.mean(values * values, axis=-1, keepdims=True) + EPSILON)


def dot(a, b, ca, cb):
    return lax.dot_general(a, b, (((ca,), (cb,)), ((), ())), preferred_element_type=f32)


def params(room=20 * MIB):
    return pltpu.CompilerParams(vmem_limit_bytes=min(room, 56 * MIB))


def turn(v, cosine, sine):
    return v * cosine + pltpu.roll(v, HD // 2, 1) * sine


def call(
    kernel, token, args, in_specs, outs, out_specs, name, takes, grid=(), scratch=(), others=(), aliases=None,
    room=20 * MIB,
):
    waits = [*([] if token is None else [token]), *others]
    unread = pl.BlockSpec(memory_space=pl.ANY)
    count = len(args)

    def body(*refs):
        rest = refs[count + len(waits) :]
        kernel(*refs[:count], *rest[: len(outs)], *rest[len(outs) + 1 :])

    return pl.pallas_call(
        body,
        grid=grid,
        in_specs=[*in_specs, *[unread] * len(waits)],
        out_specs=[*out_specs, unread],
        out_shape=[*outs, jax.ShapeDtypeStruct((8, 128), f32)],
        scratch_shapes=list(scratch),
        input_output_aliases=aliases or {},
        compiler_params=params(room),
        cost_estimate=hint(takes),
        name=name,
    )(*args, *waits)


def like(*shape, dtype=bf16):
    return jax.ShapeDtypeStruct(shape, dtype)


def rope_kernel(q_cols, k_cols, raw_ref, cos_ref, sin_ref, q_ref, kv_ref):
    cosine, sine = cos_ref[...], sin_ref[...]
    for c in range(0, q_cols, HD):
        q_ref[:, c : c + HD] = turn(raw_ref[:, c : c + HD], cosine, sine).astype(bf16)
    for c in range(0, k_cols, HD):
        v = raw_ref[:, q_cols + c : q_cols + c + HD]
        kv_ref[:, c : c + HD] = turn(v, cosine, sine).astype(bf16)
    kv_ref[:, k_cols:] = raw_ref[:, q_cols + k_cols :].astype(bf16)


def rope(raw, cosine, sine, rows, q_cols, k_cols, token=None):
    total, width = raw.shape
    table = pl.BlockSpec((rows, HD), lambda i: (0, 0))
    return call(
        functools.partial(rope_kernel, q_cols, k_cols),
        token,
        (raw, cosine, sine),
        [pl.BlockSpec((rows, width), lambda i: (i, 0)), table, table],
        [like(total, q_cols), like(total, 2 * k_cols)],
        [
            pl.BlockSpec((rows, q_cols), lambda i: (i, 0)),
            pl.BlockSpec((rows, 2 * k_cols), lambda i: (i, 0)),
        ],
        "rope",
        2,
        grid=(total // rows,),
    )


def heads_to_rows(block, kv, group):
    return jnp.concatenate(
        [block[:, (kv * group + g) * HD : (kv * group + g + 1) * HD] for g in range(group)], axis=0
    )


def keys_of(near_ref, far_ref, c):
    parts = [r[:, 0, :, c : c + HD].reshape(-1, HD) for r in (near_ref, far_ref)]
    return jnp.concatenate(parts, axis=0)


def attend_kernel(local_kv, group, q_ref, near_ref, far_ref, qpos_ref, kpos_ref, out_ref, log_ref):
    rows = q_ref.shape[0]
    allowed = kpos_ref[...] <= qpos_ref[...]
    for kv in range(local_kv):
        q = heads_to_rows(q_ref, kv, group)
        keys = keys_of(near_ref, far_ref, kv * HD)
        values = keys_of(near_ref, far_ref, (local_kv + kv) * HD)
        s = jnp.where(allowed, dot(q, keys, 1, 1) * (HD**-0.5), NEGATIVE)
        top = jnp.max(s, axis=-1, keepdims=True)
        e = jnp.exp(s - top)
        total = jnp.sum(e, axis=-1, keepdims=True)
        probs = (e * (1.0 / total)).astype(bf16)
        out = dot(probs, values, 1, 0)
        for g in range(group):
            c = (kv * group + g) * HD
            out_ref[:, c : c + HD] = out[g * rows : (g + 1) * rows].astype(bf16)
        log_ref[kv] = top + jnp.log(total)


def score_room(kpos, qpos):
    return 4 * MIB + 14 * 4 * kpos.size * qpos.size


def attend(q, near, far, qpos, kpos, rows, local_kv, group):
    total, width = q.shape
    seqs = total // rows
    blocks, _, _, kv_width = near.shape
    kv_spec = pl.BlockSpec((blocks, 1, rows, kv_width), lambda i: (0, i, 0, 0))
    return pl.pallas_call(
        functools.partial(attend_kernel, local_kv, group),
        grid=(seqs,),
        in_specs=[
            pl.BlockSpec((rows, width), lambda i: (i, 0)),
            kv_spec,
            kv_spec,
            pl.BlockSpec(qpos.shape, lambda i: (0, 0)),
            pl.BlockSpec(kpos.shape, lambda i: (0, 0)),
        ],
        out_specs=[
            pl.BlockSpec((rows, width), lambda i: (i, 0)),
            pl.BlockSpec((local_kv, group * rows, 1), lambda i: (i, 0, 0)),
        ],
        out_shape=[
            jax.ShapeDtypeStruct((total, width), bf16),
            jax.ShapeDtypeStruct((seqs * local_kv, group * rows, 1), f32),
        ],
        compiler_params=params(score_room(kpos, qpos)),
        cost_estimate=hint(9),
        name="attend",
    )(q, near, far, qpos, kpos)


def attend_back_kernel(
    local_kv, group, q_ref, near_ref, far_ref, qpos_ref, kpos_ref, log_ref, grad_ref, cos_ref, sin_ref,
    dq_ref, dnear_ref, dfar_ref,
):
    rows = q_ref.shape[0]
    half = near_ref.shape[0] * rows
    scale = HD**-0.5
    allowed = kpos_ref[...] <= qpos_ref[...]
    cosine, sine = cos_ref[...], sin_ref[...]
    for kv in range(local_kv):
        ck, cv = kv * HD, (local_kv + kv) * HD
        q = heads_to_rows(q_ref, kv, group)
        grad = heads_to_rows(grad_ref, kv, group)
        keys = keys_of(near_ref, far_ref, ck)
        values = keys_of(near_ref, far_ref, cv)
        s = jnp.where(allowed, dot(q, keys, 1, 1) * scale, NEGATIVE)
        probs = jnp.exp(s - log_ref[kv])
        prob_grad = dot(grad, values, 1, 1)
        both = probs * prob_grad
        delta = jnp.sum(both, axis=-1, keepdims=True)
        ds = (both - probs * delta).astype(bf16)
        dq = dot(ds, keys, 1, 0) * scale
        for g in range(group):
            c = (kv * group + g) * HD
            dq_ref[:, c : c + HD] = turn(dq[g * rows : (g + 1) * rows], cosine, -sine).astype(bf16)
        dk = (dot(ds, q, 0, 0) * scale).astype(bf16)
        dv = dot(probs.astype(bf16), grad, 0, 0).astype(bf16)
        for d, c in ((dk, ck), (dv, cv)):
            dnear_ref[:, 0, :, c : c + HD] = d[:half].reshape(-1, rows, HD)
            dfar_ref[:, 0, :, c : c + HD] = d[half:].reshape(-1, rows, HD)


def attend_back(
    q, near, far, qpos, kpos, log, grad, cosine, sine, rows, local_kv, group, token, others
):
    total, width = q.shape
    blocks, _, _, kv_width = near.shape
    kv_spec = pl.BlockSpec((blocks, 1, rows, kv_width), lambda i: (0, i, 0, 0))
    row_spec = pl.BlockSpec((rows, width), lambda i: (i, 0))
    table = pl.BlockSpec((rows, HD), lambda i: (0, 0))
    return call(
        functools.partial(attend_back_kernel, local_kv, group),
        token,
        (q, near, far, qpos, kpos, log, grad, cosine, sine),
        [
            row_spec,
            kv_spec,
            kv_spec,
            pl.BlockSpec(qpos.shape, lambda i: (0, 0)),
            pl.BlockSpec(kpos.shape, lambda i: (0, 0)),
            pl.BlockSpec((local_kv, group * rows, 1), lambda i: (i, 0, 0)),
            row_spec,
            table,
            table,
        ],
        [like(total, width), like(*near.shape), like(*far.shape)],
        [row_spec, kv_spec, kv_spec],
        "attend_back",
        13,
        grid=(total // rows,),
        others=others,
        room=score_room(kpos, qpos),
    )


def arrange_kernel(block, order_ref, a_ref, keep_ref, send_ref):
    half = order_ref.shape[0] // 2
    for j in range(half):
        for out_ref, at in ((keep_ref, j), (send_ref, half + j)):
            start = pl.multiple_of(order_ref[at] * block, block)
            out_ref[:, j * block : (j + 1) * block] = a_ref[:, pl.ds(start, block)]


def arrange(a, order):
    rows, width = a.shape
    count = order.shape[0]
    block = width // count
    if block % 128:
        moved = jnp.take(a.reshape(rows, count, block), order, axis=1).reshape(rows, width)
        return moved[:, : width // 2], moved[:, width // 2 :]
    out = jax.ShapeDtypeStruct((rows, width // 2), a.dtype)
    return pl.pallas_call(
        functools.partial(arrange_kernel, block),
        in_specs=[
            pl.BlockSpec(memory_space=pltpu.SMEM),
            pl.BlockSpec(memory_space=pltpu.VMEM),
        ],
        out_specs=[pl.BlockSpec(memory_space=pltpu.VMEM)] * 2,
        out_shape=[out, out],
        compiler_params=params(),
        cost_estimate=hint(1),
        name="arrange",
    )(order, a)


def forward_kernel(hidden_ref, gate_w_ref, up_w_ref, *refs):
    gate_ref, up_ref, product_ref = refs[-3:]
    hidden = hidden_ref[...]
    gate = dot(hidden, gate_w_ref[...], 1, 0)
    up = dot(hidden, up_w_ref[...], 1, 0)
    gate_ref[...] = gate
    up_ref[...] = up
    product_ref[...] = (gate * jax.nn.sigmoid(gate) * up).astype(bf16)


def feed_forward(hidden, weights, units, columns, before, token):
    rows, width = hidden.shape
    start, count = columns
    tile = math.gcd(math.gcd(start, count), math.gcd(units, 256))
    tiles, first = units // tile, start // tile
    column = pl.BlockSpec((rows, tile), lambda i: (0, first + i))
    return call(
        forward_kernel,
        token,
        (hidden, weights, weights, *before),
        [
            pl.BlockSpec((rows, width), lambda i: (0, 0)),
            pl.BlockSpec((width, tile), lambda i: (0, first + i)),
            pl.BlockSpec((width, tile), lambda i: (0, tiles + first + i)),
            *[pl.BlockSpec(memory_space=pl.ANY)] * len(before),
        ],
        [like(rows, units, dtype=f32), like(rows, units, dtype=f32), like(rows, count)],
        [column, column, pl.BlockSpec((rows, tile), lambda i: (0, i))],
        "feed_forward",
        17 * count / units,
        grid=(count // tile,),
        aliases={3: 0, 4: 1} if before else None,
    )


def backward_kernel(
    down_grad_ref, gate_ref, up_ref, gate_w_ref, up_w_ref, down_w_ref, grads_ref, partial_ref, sum_ref
):
    product_grad = dot(down_grad_ref[...], down_w_ref[...], 1, 0)
    gate, up = gate_ref[...], up_ref[...]
    sigmoid = jax.nn.sigmoid(gate)
    gate_grad = (product_grad * up * (sigmoid * (1.0 + gate * (1.0 - sigmoid)))).astype(bf16)
    up_grad = (product_grad * gate * sigmoid).astype(bf16)
    grads_ref[0] = gate_grad
    grads_ref[1] = up_grad
    term = dot(gate_grad, gate_w_ref[...], 1, 1) + dot(up_grad, up_w_ref[...], 1, 1)

    @pl.when(pl.program_id(0) == 0)
    def _():
        sum_ref[...] = term

    @pl.when(pl.program_id(0) != 0)
    def _():
        sum_ref[...] += term

    @pl.when(pl.program_id(0) == pl.num_programs(0) - 1)
    def _():
        partial_ref[...] = sum_ref[...].astype(bf16)


def feed_forward_back(down_grad, gate, up, weights, units, token):
    rows, width = down_grad.shape
    tile = math.gcd(units, 256)
    tiles = units // tile
    whole = pl.BlockSpec((rows, width), lambda i: (0, 0))
    column = pl.BlockSpec((rows, tile), lambda i: (0, i))
    return call(
        backward_kernel,
        token,
        (down_grad, gate, up, weights, weights, weights),
        [
            whole,
            column,
            column,
            pl.BlockSpec((width, tile), lambda i: (0, i)),
            pl.BlockSpec((width, tile), lambda i: (0, tiles + i)),
            pl.BlockSpec((width, tile), lambda i: (0, 2 * tiles + i)),
        ],
        [like(2, rows, units), like(rows, width)],
        [pl.BlockSpec((2, rows, tile), lambda i: (0, 0, i)), whole],
        "feed_forward_back",
        28,
        grid=(tiles,),
        scratch=[pltpu.VMEM((rows, width), f32)],
    )


def turned_kernel(a_ref, w_ref, out_ref):
    out_ref[...] = dot(a_ref[...], w_ref[...], 1, 1).astype(bf16)


def times_turned(a, weights, at, token):
    rows, depth = a.shape
    height = weights.shape[0]
    tile = math.gcd(height, 256)
    return call(
        turned_kernel,
        token,
        (a, weights),
        [
            pl.BlockSpec((rows, depth), lambda i: (0, 0)),
            pl.BlockSpec((tile, depth), lambda i: (i, at)),
        ],
        [like(rows, height)],
        [pl.BlockSpec((rows, tile), lambda i: (0, i))],
        "times_turned",
        9,
        grid=(height // tile,),
        room=48 * MIB,
    )


def product_kernel(blocks, a_ref, a2_ref, b_ref, b2_ref, *out_refs):
    for out_ref, chosen in zip(out_refs, blocks, strict=True):
        sides = []
        for ref in (a_ref, a2_ref):
            parts = [ref[:, start:end] for start, end in chosen]
            sides.append(parts[0] if len(parts) == 1 else jnp.concatenate(parts, axis=1))
        out = dot(sides[0], b_ref[...], 0, 0) + dot(sides[1], b2_ref[...], 0, 0)
        out_ref[...] = out.astype(bf16)


def side_products(side, b, b2, which, columns, blocks, token):
    a, a2 = side
    rows, width = a.shape
    start, count = columns
    tile = 768 if math.gcd(start, count) % 768 == 0 else math.gcd(start, count)
    first = start // tile
    whole = pl.BlockSpec((rows, width), lambda i: (0, 0))
    b_spec = pl.BlockSpec((None, rows, tile), lambda i: (which, 0, first + i))
    return call(
        functools.partial(product_kernel, blocks),
        token,
        (a, a2, b, b2),
        [whole, whole, b_spec, b_spec],
        [like(width // 2, count)] * 2,
        [pl.BlockSpec((width // 2, tile), lambda i: (0, i))] * 2,
        "side_products",
        6,
        grid=(count // tile,),
    )


def fold_kernel(kept_ref, received_ref, *out_refs):
    height = out_refs[0].shape[0]
    for i, out_ref in enumerate(out_refs):
        part = slice(i * height, (i + 1) * height)
        out = kept_ref[part].astype(f32) + received_ref[part].astype(f32)
        out_ref[...] = out.astype(out_ref.dtype)


def fold(kept, received, last, token):
    rows, width = kept.shape
    whole = pl.BlockSpec(memory_space=pltpu.VMEM)
    outs = [like(rows, width, dtype=f32)] if last else [like(rows // 2, width, dtype=kept.dtype)] * 2
    return call(
        fold_kernel, token, (kept, received), [whole] * 2, outs, [whole] * len(outs), "fold", 1.5,
        room=max(20 * MIB, 4 * MIB + 4 * kept.size * kept.dtype.itemsize),
    )


def hold_kernel(*refs):
    pass


def hold(v, token):
    anywhere = pl.BlockSpec(memory_space=pl.ANY)
    out = like(*v.shape, dtype=v.dtype)
    return call(
        hold_kernel, token, (v,), [anywhere], [out], [anywhere], "hold", 0.1, aliases={0: 0}
    )


def norm_back_kernel(
    mine_ref, theirs_ref, v_ref, gain_ref, base_ref, grad_ref, low_ref, gain_grad_ref
):
    hidden_grad = mine_ref[...].astype(f32) + theirs_ref[...].astype(f32)
    v = v_ref[...].astype(f32)
    scale = rms_scale(v)
    normed = v * scale
    gain_grad = jnp.sum(hidden_grad * normed, axis=0, keepdims=True)

    @pl.when(pl.program_id(0) == 0)
    def _():
        gain_grad_ref[...] = gain_grad

    @pl.when(pl.program_id(0) != 0)
    def _():
        gain_grad_ref[...] += gain_grad

    g = hidden_grad * gain_ref[...]
    out = base_ref[...].astype(f32) + scale * (
        g - normed * jnp.mean(g * normed, axis=-1, keepdims=True)
    )
    grad_ref[...] = out
    low_ref[...] = out.astype(bf16)


def norm_back(mine, theirs, v, gain, base, rows, token):
    total, width = mine.shape
    spec = pl.BlockSpec((rows, width), lambda i: (i, 0))
    row = pl.BlockSpec((1, width), lambda i: (0, 0))
    return call(
        norm_back_kernel,
        token,
        (mine, theirs, v, gain, base),
        [spec, spec, spec, row, spec],
        [like(total, width, dtype=f32), like(total, width), like(1, width, dtype=f32)],
        [spec, spec, row],
        "norm_back",
        6.5,
        grid=(total // rows,),
    )


def local(
    n_dp,
    tokens,
    cotangent,
    active,
    assignment,
    attention_gain,
    query_weight,
    key_weight,
    value_weight,
    out_weight,
    feedforward_gain,
    gate_weight,
    up_weight,
    down_weight,
):
    rows, width = tokens.shape[1:]
    live_seqs = tokens.shape[0] - 1
    total = live_seqs * rows
    block = width // n_dp
    groups = n_dp // 4
    q_cols, k_cols = query_weight.shape[1], key_weight.shape[1]
    hidden_units = gate_weight.shape[1]
    local_kv = k_cols // HD
    group = q_cols // k_cols
    me = lax.axis_index("dp").astype(jnp.int32)

    def flip(v, bits):
        return lax.ppermute(v, "dp", [(i, i ^ bits) for i in range(n_dp)])

    def tensor_flip(v):
        return lax.ppermute(v, "tensor", [(0, 1), (1, 0)])

    def tensor_total(partial_rows):
        mine = lax.optimization_barrier(partial_rows.astype(bf16))
        return mine.astype(f32) + tensor_flip(mine).astype(f32)

    far_bits = [1 << b for b in range(groups.bit_length() - 1)]
    fars = [0]
    for bit in reversed(far_bits):
        fars = fars + [far + bit for far in fars]
    near_places = [far * 4 + pair * 2 for pair in range(2) for far in fars]
    places = near_places + [place + 1 for place in near_places]
    owners = jnp.bitwise_xor(me, jnp.asarray(places, jnp.int32))

    positions = me * rows + jnp.arange(rows, dtype=jnp.int32)
    frequency = jnp.exp(
        -jnp.log(10000.0) * (2.0 * jnp.arange(HD // 2, dtype=f32) / HD)
    )
    angles = positions.astype(f32)[:, None] * frequency[None, :]
    cosine = jnp.concatenate([jnp.cos(angles)] * 2, axis=1)
    sine = jnp.concatenate([-jnp.sin(angles), jnp.sin(angles)], axis=1)
    qpos = jnp.tile(positions, group)[:, None]
    kpos = (owners[:, None] * rows + jnp.arange(rows, dtype=jnp.int32)[None, :]).reshape(1, -1)

    gains = jnp.stack([attention_gain, feedforward_gain], axis=1)
    gains = jnp.pad(gains, ((0, 0), (0, 126)))
    first = lax.all_gather(
        jnp.concatenate([query_weight, key_weight, value_weight, out_weight.T, gains], axis=1),
        "dp", axis=0, tiled=True,
    )
    second = lax.all_gather(
        jnp.concatenate([gate_weight, up_weight, down_weight.T], axis=1), "dp", axis=0, tiled=True
    )
    down_turned = second[:, 2 * hidden_units :]
    qkv_cols = q_cols + 2 * k_cols
    qkv_full = first[:, :qkv_cols]
    out_turned = first[:, qkv_cols : qkv_cols + q_cols]
    gain_attn_row = first[:, qkv_cols + q_cols].astype(f32)[None, :]
    gain_mlp = first[:, qkv_cols + q_cols + 1].astype(f32)[None, :]

    dead_slot = jnp.argmin(active.reshape(-1))
    dead = assignment[dead_slot]
    is_dead = (jnp.arange(live_seqs, dtype=jnp.int32) == dead)[:, None, None]

    def pick(v):
        return jnp.where(is_dead, v[live_seqs:], v[:live_seqs]).reshape(total, width)

    def unpick(live_values, skipped):
        live_values = live_values.reshape(live_seqs, rows, width)
        last = lax.dynamic_slice_in_dim(live_values, jnp.minimum(dead, live_seqs - 1), 1, 0)
        return jnp.concatenate(
            [
                jnp.where(is_dead, skipped[:live_seqs], live_values),
                jnp.where(dead == live_seqs, skipped[live_seqs:], last),
            ],
            axis=0,
        )

    token_low = lax.optimization_barrier(pick(tokens))
    token_rows = token_low.astype(f32)
    down_grad = lax.optimization_barrier(pick(cotangent))

    hidden = (token_rows * rms_scale(token_rows) * gain_attn_row).astype(bf16)
    qkv_raw = dot(hidden, qkv_full, 1, 0)
    queries, kv_own, _ = rope(qkv_raw, cosine, sine, rows, q_cols, k_cols)
    kv_own = kv_own.reshape(1, live_seqs, rows, 2 * k_cols)
    kv_near = kv_own
    for bits in [4 * bit for bit in reversed(far_bits)] + [2]:
        kv_near = jnp.concatenate([kv_near, flip(kv_near, bits)], axis=0)
    kv_other = flip(kv_near, 1)
    mixed_out, log_total = attend(
        queries, kv_near, kv_other, qpos, kpos, rows, local_kv, group
    )
    branch = tensor_total(dot(mixed_out, out_turned, 1, 1))
    middle = token_rows + branch

    hidden_mlp = (middle * rms_scale(middle) * gain_mlp).astype(bf16)
    def side(a):
        keep, send = arrange(a, owners)
        return keep, flip(send, 1)

    token = [None]

    def run(kernel, *args, **kwargs):
        *outs, token[0] = kernel(*args, **kwargs, token=token[0])
        return outs if len(outs) > 1 else outs[0]

    class Total:
        def __init__(self, kept, received, bits):
            self.kept, self.received, self.bits, self.out = kept, received, list(bits), None

        def step(self):
            if self.out is not None:
                return
            if not self.bits:
                self.out = run(fold, self.kept, self.received, True)
                return
            self.kept, sent = run(fold, self.kept, self.received, False)
            self.received = flip(sent, self.bits.pop(0))

        def end(self):
            while self.out is None:
                self.step()
            return self.out

    far_flips = [4 * bit for bit in far_bits]
    far_first = FAR_FIRST if block % 128 == 0 else ()

    def weight_total(name, *args):
        if name in far_first:
            places = [pair * groups + far for far in range(groups) for pair in range(2)]
            spans = [(place * block, (place + 1) * block) for place in places]
            blocks, bits = [spans[:groups], spans[groups:]], [*far_flips, 2]
        else:
            half = groups * block
            blocks, bits = [[(0, half)], [(half, 2 * half)]], [2, *far_flips]
        kept, sent = run(side_products, *args, blocks)
        return Total(kept, flip(sent, bits[0]), bits[1:])

    split_at = -(-hidden_units // 512) * 256
    columns = ((0, split_at), (split_at, hidden_units - split_at))
    down_side, mlp_side, attn_side = side(down_grad), side(hidden_mlp), side(hidden)
    mixed2 = flip(mixed_out, 1)
    arrived = [down_side[1], mlp_side[1], attn_side[1], mixed2]
    (token[0],) = call(hold_kernel, None, (), [], [], [], "hold", 0.1, others=arrived)

    totals, made = {}, {}
    kv_cols = 2 * k_cols
    chunks = {"A": columns[0], "B": columns[1]}

    def send_products(name):
        if name[0] == "d":
            product, product2 = made["product" + name[1]]
            args = (down_side, product[None], product2[None], 0, (0, product.shape[1]))
        elif name[0] in "gu":
            which = "gu".index(name[0])
            args = (mlp_side, made["grads"], made["grads2"], which, chunks[name[1]])
        elif name == "q":
            args = (attn_side, made["qkv_grad"][None], made["qkv_grad2"][None], 0, (0, qkv_cols))
        else:
            args = (made["out_side"], mixed_out[None], mixed2[None], 0, (0, q_cols))
        totals[name] = weight_total(name, *args)

    def feed(name):
        before = made.get("gate_up", ())
        *made["gate_up"], product = run(
            feed_forward, hidden_mlp, second, hidden_units, chunks[name], before
        )
        made["product" + name] = product, flip(product, 1)

    def feed_back():
        made["grads"], made["partial"] = run(
            feed_forward_back, down_grad, *made["gate_up"], second, hidden_units
        )

    def exchange():
        grads, partial = run(hold, made["grads"]), run(hold, made["partial"])
        made.update(grads=grads, grads2=flip(grads, 1), partial=partial, theirs=tensor_flip(partial))

    def middle_back():
        made["middle_grad"], made["branch_grad"], made["gain_mlp"] = run(
            norm_back, made["partial"], made["theirs"], middle, gain_mlp, down_grad, rows
        )

    def mixed_back():
        made["out_side"] = side(made["branch_grad"])
        made["mixed_grad"] = dot(made["branch_grad"], out_turned, 1, 0).astype(bf16)

    def attention_back():
        mixed_grad = made["mixed_grad"]
        made["query_grad"], made["near"], made["other"] = run(
            attend_back, queries, kv_near, kv_other, qpos, kpos, log_total, mixed_grad,
            cosine, sine, rows, local_kv, group, others=[made["out_side"][1]],
        )

    def keys_back():
        other = run(hold, made["other"])
        totals["k"] = Total(
            made["near"].reshape(-1, kv_cols), flip(other.reshape(-1, kv_cols), 1), [2, *far_flips]
        )

    def turn_back():
        dkv = totals["k"].end()
        key_grad, _ = run(
            rope, jnp.concatenate([dkv[:, :k_cols], dkv], axis=1), cosine, -sine, rows, k_cols, k_cols
        )
        qkv_grad = jnp.concatenate(
            [made["query_grad"], key_grad, dkv[:, k_cols:].astype(bf16)], axis=1
        )
        made.update(qkv_grad=qkv_grad, qkv_grad2=flip(qkv_grad, 1))

    def attention_partial():
        made["attn"] = run(times_turned, made["qkv_grad"], first, 0)
        made["attn_theirs"] = tensor_flip(made["attn"])

    def input_back():
        made["input_grad"], _, gain_attn = run(
            norm_back, made["attn"], made["attn_theirs"], token_low, gain_attn_row,
            made["middle_grad"], rows,
        )
        gains = jnp.concatenate([gain_attn, made["gain_mlp"]]).reshape(2, n_dp, block)
        gains = jnp.take(gains, owners, axis=1).transpose(1, 0, 2).reshape(n_dp, 2 * block)
        totals["n"] = Total(gains[: 2 * groups], flip(gains[2 * groups :], 1), [2, *far_flips])

    def down_value():
        product = jnp.concatenate([made["product" + name][0] for name in "AB"], axis=1)
        made["down"] = run(times_turned, product, second, 2)
        made["down_theirs"] = tensor_flip(made["down"])

    actions = {
        "F": feed_back, "H": exchange, "N": middle_back, "M": mixed_back, "A": attention_back, "K": keys_back,
        "R": turn_back, "T": attention_partial, "I": input_back, "V": down_value,
    }
    for entry in ORDER:
        if entry in actions:
            actions[entry]()
        elif entry[0] == "f":
            feed(entry[1])
        elif entry[0] == "P":
            send_products(entry[1:])
        else:
            totals[entry[1:]].step()
    finished = {name: v.end() for name, v in totals.items()}
    down_partial, down_theirs = made["down"], made["down_theirs"]
    input_grad, gains, grad_out, grad_qkv = (
        made["input_grad"], finished["n"], finished["o"], finished["q"],
    )
    grad_down, grad_gate, grad_up = [[finished[m + c] for c in "AB"] for m in "dgu"]
    down_values = down_partial.astype(f32) + down_theirs.astype(f32)
    result = unpick((middle + down_values).astype(bf16), tokens)
    input_grad = unpick(input_grad, cotangent.astype(f32))

    return (
        result,
        input_grad,
        gains[0, :block],
        grad_qkv[:, :q_cols],
        grad_qkv[:, q_cols : q_cols + k_cols],
        grad_qkv[:, q_cols + k_cols :],
        grad_out.T,
        gains[0, block:],
        jnp.concatenate(grad_gate, axis=1),
        jnp.concatenate(grad_up, axis=1),
        jnp.concatenate(grad_down, axis=1).T,
    )


def solution(mesh):
    rows = P(None, "dp", None)
    split = P("dp", "tensor")
    turned = P("tensor", "dp")
    gain = P("dp")
    weights = (gain, split, split, split, turned, gain, split, split, turned)
    return jax.shard_map(
        functools.partial(local, mesh.shape["dp"]),
        mesh=mesh,
        in_specs=(rows, rows, P(), P(), *weights),
        out_specs=(rows, rows, *weights),
        check_vma=False,
    )
```

```python
import functools
import math

import jax
import jax.numpy as jnp
from jax import lax
from jax.experimental import pallas as pl
from jax.experimental.pallas import tpu as pltpu
from jax.sharding import PartitionSpec as P

HD = 128
EPSILON = 1e-05
NEGATIVE = -1e30
MIB = 1024 * 1024


def hint(microseconds):
    return pl.CostEstimate(
        flops=int(microseconds * 3.5e8), bytes_accessed=int(microseconds * 1.26e6), transcendentals=0
    )


FAR_FIRST = ("o",)
ORDER = (
    "fA", "fB", "PdA", "PdB", "F", "SdA", "H", "PgA", "SdB", "N", "SdA", "M", "A", "SgA", "SdB",
    "K", "PgB", "Sk", "V", "SdA", "SdA", "Sk", "SgA", "PuA", "SgB", "Sk", "SdB", "Sk", "R",
    "Po", "SgB", "Pq", "T", "SuA", "PuB", "So", "SgA", "Sq", "I", "SuA", "So", "SgB", "Sq",
    "SuA", "SuB", "So", "Sn", "Sq", "Sn", "SuB", "Sn", "SuB", "Sn",
)

bf16 = jnp.bfloat16
f32 = jnp.float32


def rms_scale(values):
    return lax.rsqrt(jnp.mean(values * values, axis=-1, keepdims=True) + EPSILON)


def dot(a, b, ca, cb):
    return lax.dot_general(a, b, (((ca,), (cb,)), ((), ())), preferred_element_type=f32)


def params(room=16 * MIB):
    return pltpu.CompilerParams(vmem_limit_bytes=min(room, 56 * MIB))


def turn(v, cosine, sine):
    return v * cosine + pltpu.roll(v, HD // 2, 1) * sine


def call(
    kernel, token, args, in_specs, outs, out_specs, name, takes, grid=(), scratch=(), others=(), aliases=None,
    room=16 * MIB,
):
    waits = [*([] if token is None else [token]), *others]
    unread = pl.BlockSpec(memory_space=pl.ANY)
    count = len(args)

    def body(*refs):
        rest = refs[count + len(waits) :]
        kernel(*refs[:count], *rest[: len(outs)], *rest[len(outs) + 1 :])

    return pl.pallas_call(
        body,
        grid=grid,
        in_specs=[*in_specs, *[unread] * len(waits)],
        out_specs=[*out_specs, unread],
        out_shape=[*outs, jax.ShapeDtypeStruct((8, 128), f32)],
        scratch_shapes=list(scratch),
        input_output_aliases=aliases or {},
        compiler_params=params(room),
        cost_estimate=hint(takes),
        name=name,
    )(*args, *waits)


def like(*shape, dtype=bf16):
    return jax.ShapeDtypeStruct(shape, dtype)


def rope_kernel(q_cols, k_cols, raw_ref, cos_ref, sin_ref, q_ref, kv_ref):
    cosine, sine = cos_ref[...], sin_ref[...]
    for c in range(0, q_cols, HD):
        q_ref[:, c : c + HD] = turn(raw_ref[:, c : c + HD], cosine, sine).astype(bf16)
    for c in range(0, k_cols, HD):
        v = raw_ref[:, q_cols + c : q_cols + c + HD]
        kv_ref[:, c : c + HD] = turn(v, cosine, sine).astype(bf16)
    kv_ref[:, k_cols:] = raw_ref[:, q_cols + k_cols :].astype(bf16)


def rope(raw, cosine, sine, rows, q_cols, k_cols, token=None):
    total, width = raw.shape
    table = pl.BlockSpec((rows, HD), lambda i: (0, 0))
    return call(
        functools.partial(rope_kernel, q_cols, k_cols),
        token,
        (raw, cosine, sine),
        [pl.BlockSpec((rows, width), lambda i: (i, 0)), table, table],
        [like(total, q_cols), like(total, 2 * k_cols)],
        [
            pl.BlockSpec((rows, q_cols), lambda i: (i, 0)),
            pl.BlockSpec((rows, 2 * k_cols), lambda i: (i, 0)),
        ],
        "rope",
        2,
        grid=(total // rows,),
    )


def heads_to_rows(block, kv, group):
    return jnp.concatenate(
        [block[:, (kv * group + g) * HD : (kv * group + g + 1) * HD] for g in range(group)], axis=0
    )


def keys_of(near_ref, far_ref, c):
    parts = [r[:, 0, :, c : c + HD].reshape(-1, HD) for r in (near_ref, far_ref)]
    return jnp.concatenate(parts, axis=0)


def attend_kernel(local_kv, group, q_ref, near_ref, far_ref, qpos_ref, kpos_ref, out_ref, log_ref):
    rows = q_ref.shape[0]
    allowed = kpos_ref[...] <= qpos_ref[...]
    for kv in range(local_kv):
        q = heads_to_rows(q_ref, kv, group)
        keys = keys_of(near_ref, far_ref, kv * HD)
        values = keys_of(near_ref, far_ref, (local_kv + kv) * HD)
        s = jnp.where(allowed, dot(q, keys, 1, 1) * (HD**-0.5), NEGATIVE)
        top = jnp.max(s, axis=-1, keepdims=True)
        e = jnp.exp(s - top)
        total = jnp.sum(e, axis=-1, keepdims=True)
        probs = (e * (1.0 / total)).astype(bf16)
        out = dot(probs, values, 1, 0)
        for g in range(group):
            c = (kv * group + g) * HD
            out_ref[:, c : c + HD] = out[g * rows : (g + 1) * rows].astype(bf16)
        log_ref[kv] = top + jnp.log(total)


def score_room(kpos, qpos):
    return 4 * MIB + 14 * 4 * kpos.size * qpos.size


def attend(q, near, far, qpos, kpos, rows, local_kv, group):
    total, width = q.shape
    seqs = total // rows
    blocks, _, _, kv_width = near.shape
    kv_spec = pl.BlockSpec((blocks, 1, rows, kv_width), lambda i: (0, i, 0, 0))
    return pl.pallas_call(
        functools.partial(attend_kernel, local_kv, group),
        grid=(seqs,),
        in_specs=[
            pl.BlockSpec((rows, width), lambda i: (i, 0)),
            kv_spec,
            kv_spec,
            pl.BlockSpec(qpos.shape, lambda i: (0, 0)),
            pl.BlockSpec(kpos.shape, lambda i: (0, 0)),
        ],
        out_specs=[
            pl.BlockSpec((rows, width), lambda i: (i, 0)),
            pl.BlockSpec((local_kv, group * rows, 1), lambda i: (i, 0, 0)),
        ],
        out_shape=[
            jax.ShapeDtypeStruct((total, width), bf16),
            jax.ShapeDtypeStruct((seqs * local_kv, group * rows, 1), f32),
        ],
        compiler_params=params(score_room(kpos, qpos)),
        cost_estimate=hint(9),
        name="attend",
    )(q, near, far, qpos, kpos)


def attend_back_kernel(
    local_kv, group, q_ref, near_ref, far_ref, qpos_ref, kpos_ref, log_ref, grad_ref, cos_ref, sin_ref,
    dq_ref, dnear_ref, dfar_ref,
):
    rows = q_ref.shape[0]
    half = near_ref.shape[0] * rows
    scale = HD**-0.5
    allowed = kpos_ref[...] <= qpos_ref[...]
    cosine, sine = cos_ref[...], sin_ref[...]
    for kv in range(local_kv):
        ck, cv = kv * HD, (local_kv + kv) * HD
        q = heads_to_rows(q_ref, kv, group)
        grad = heads_to_rows(grad_ref, kv, group)
        keys = keys_of(near_ref, far_ref, ck)
        values = keys_of(near_ref, far_ref, cv)
        s = jnp.where(allowed, dot(q, keys, 1, 1) * scale, NEGATIVE)
        probs = jnp.exp(s - log_ref[kv])
        prob_grad = dot(grad, values, 1, 1)
        both = probs * prob_grad
        delta = jnp.sum(both, axis=-1, keepdims=True)
        ds = (both - probs * delta).astype(bf16)
        dq = dot(ds, keys, 1, 0) * scale
        for g in range(group):
            c = (kv * group + g) * HD
            dq_ref[:, c : c + HD] = turn(dq[g * rows : (g + 1) * rows], cosine, -sine).astype(bf16)
        dk = (dot(ds, q, 0, 0) * scale).astype(bf16)
        dv = dot(probs.astype(bf16), grad, 0, 0).astype(bf16)
        for d, c in ((dk, ck), (dv, cv)):
            dnear_ref[:, 0, :, c : c + HD] = d[:half].reshape(-1, rows, HD)
            dfar_ref[:, 0, :, c : c + HD] = d[half:].reshape(-1, rows, HD)


def attend_back(
    q, near, far, qpos, kpos, log, grad, cosine, sine, rows, local_kv, group, token, others
):
    total, width = q.shape
    blocks, _, _, kv_width = near.shape
    kv_spec = pl.BlockSpec((blocks, 1, rows, kv_width), lambda i: (0, i, 0, 0))
    row_spec = pl.BlockSpec((rows, width), lambda i: (i, 0))
    table = pl.BlockSpec((rows, HD), lambda i: (0, 0))
    return call(
        functools.partial(attend_back_kernel, local_kv, group),
        token,
        (q, near, far, qpos, kpos, log, grad, cosine, sine),
        [
            row_spec,
            kv_spec,
            kv_spec,
            pl.BlockSpec(qpos.shape, lambda i: (0, 0)),
            pl.BlockSpec(kpos.shape, lambda i: (0, 0)),
            pl.BlockSpec((local_kv, group * rows, 1), lambda i: (i, 0, 0)),
            row_spec,
            table,
            table,
        ],
        [like(total, width), like(*near.shape), like(*far.shape)],
        [row_spec, kv_spec, kv_spec],
        "attend_back",
        13,
        grid=(total // rows,),
        others=others,
        room=score_room(kpos, qpos),
    )


def arrange_kernel(block, order_ref, a_ref, keep_ref, send_ref):
    half = order_ref.shape[0] // 2
    for j in range(half):
        for out_ref, at in ((keep_ref, j), (send_ref, half + j)):
            start = pl.multiple_of(order_ref[at] * block, block)
            out_ref[:, j * block : (j + 1) * block] = a_ref[:, pl.ds(start, block)]


def arrange(a, order):
    rows, width = a.shape
    count = order.shape[0]
    block = width // count
    if block % 128:
        moved = jnp.take(a.reshape(rows, count, block), order, axis=1).reshape(rows, width)
        return moved[:, : width // 2], moved[:, width // 2 :]
    out = jax.ShapeDtypeStruct((rows, width // 2), a.dtype)
    return pl.pallas_call(
        functools.partial(arrange_kernel, block),
        in_specs=[
            pl.BlockSpec(memory_space=pltpu.SMEM),
            pl.BlockSpec(memory_space=pltpu.VMEM),
        ],
        out_specs=[pl.BlockSpec(memory_space=pltpu.VMEM)] * 2,
        out_shape=[out, out],
        compiler_params=params(),
        cost_estimate=hint(1),
        name="arrange",
    )(order, a)


def forward_kernel(hidden_ref, gate_w_ref, up_w_ref, *refs):
    gate_ref, up_ref, product_ref = refs[-3:]
    hidden = hidden_ref[...]
    gate = dot(hidden, gate_w_ref[...], 1, 0)
    up = dot(hidden, up_w_ref[...], 1, 0)
    gate_ref[...] = gate
    up_ref[...] = up
    product_ref[...] = (gate * jax.nn.sigmoid(gate) * up).astype(bf16)


def feed_forward(hidden, weights, units, columns, before, token):
    rows, width = hidden.shape
    start, count = columns
    tile = math.gcd(math.gcd(start, count), math.gcd(units, 256))
    tiles, first = units // tile, start // tile
    column = pl.BlockSpec((rows, tile), lambda i: (0, first + i))
    return call(
        forward_kernel,
        token,
        (hidden, weights, weights, *before),
        [
            pl.BlockSpec((rows, width), lambda i: (0, 0)),
            pl.BlockSpec((width, tile), lambda i: (0, first + i)),
            pl.BlockSpec((width, tile), lambda i: (0, tiles + first + i)),
            *[pl.BlockSpec(memory_space=pl.ANY)] * len(before),
        ],
        [like(rows, units, dtype=f32), like(rows, units, dtype=f32), like(rows, count)],
        [column, column, pl.BlockSpec((rows, tile), lambda i: (0, i))],
        "feed_forward",
        17 * count / units,
        grid=(count // tile,),
        aliases={3: 0, 4: 1} if before else None,
    )


def backward_kernel(
    down_grad_ref, gate_ref, up_ref, gate_w_ref, up_w_ref, down_w_ref, grads_ref, partial_ref, sum_ref
):
    product_grad = dot(down_grad_ref[...], down_w_ref[...], 1, 0)
    gate, up = gate_ref[...], up_ref[...]
    sigmoid = jax.nn.sigmoid(gate)
    gate_grad = (product_grad * up * (sigmoid * (1.0 + gate * (1.0 - sigmoid)))).astype(bf16)
    up_grad = (product_grad * gate * sigmoid).astype(bf16)
    grads_ref[0] = gate_grad
    grads_ref[1] = up_grad
    term = dot(gate_grad, gate_w_ref[...], 1, 1) + dot(up_grad, up_w_ref[...], 1, 1)

    @pl.when(pl.program_id(0) == 0)
    def _():
        sum_ref[...] = term

    @pl.when(pl.program_id(0) != 0)
    def _():
        sum_ref[...] += term

    @pl.when(pl.program_id(0) == pl.num_programs(0) - 1)
    def _():
        partial_ref[...] = sum_ref[...].astype(bf16)


def feed_forward_back(down_grad, gate, up, weights, units, token):
    rows, width = down_grad.shape
    tile = math.gcd(units, 256)
    tiles = units // tile
    whole = pl.BlockSpec((rows, width), lambda i: (0, 0))
    column = pl.BlockSpec((rows, tile), lambda i: (0, i))
    return call(
        backward_kernel,
        token,
        (down_grad, gate, up, weights, weights, weights),
        [
            whole,
            column,
            column,
            pl.BlockSpec((width, tile), lambda i: (0, i)),
            pl.BlockSpec((width, tile), lambda i: (0, tiles + i)),
            pl.BlockSpec((width, tile), lambda i: (0, 2 * tiles + i)),
        ],
        [like(2, rows, units), like(rows, width)],
        [pl.BlockSpec((2, rows, tile), lambda i: (0, 0, i)), whole],
        "feed_forward_back",
        28,
        grid=(tiles,),
        scratch=[pltpu.VMEM((rows, width), f32)],
    )


def turned_kernel(a_ref, w_ref, out_ref):
    out_ref[...] = dot(a_ref[...], w_ref[...], 1, 1).astype(bf16)


def times_turned(a, weights, at, token):
    rows, depth = a.shape
    height = weights.shape[0]
    tile = math.gcd(height, 256)
    return call(
        turned_kernel,
        token,
        (a, weights),
        [
            pl.BlockSpec((rows, depth), lambda i: (0, 0)),
            pl.BlockSpec((tile, depth), lambda i: (i, at)),
        ],
        [like(rows, height)],
        [pl.BlockSpec((rows, tile), lambda i: (0, i))],
        "times_turned",
        9,
        grid=(height // tile,),
        room=48 * MIB,
    )


def product_kernel(blocks, a_ref, a2_ref, b_ref, b2_ref, *out_refs):
    for out_ref, chosen in zip(out_refs, blocks, strict=True):
        sides = []
        for ref in (a_ref, a2_ref):
            parts = [ref[:, start:end] for start, end in chosen]
            sides.append(parts[0] if len(parts) == 1 else jnp.concatenate(parts, axis=1))
        out = dot(sides[0], b_ref[...], 0, 0) + dot(sides[1], b2_ref[...], 0, 0)
        out_ref[...] = out.astype(bf16)


def side_products(side, b, b2, which, columns, blocks, token):
    a, a2 = side
    rows, width = a.shape
    start, count = columns
    tile = 768 if math.gcd(start, count) % 768 == 0 else math.gcd(start, count)
    first = start // tile
    whole = pl.BlockSpec((rows, width), lambda i: (0, 0))
    b_spec = pl.BlockSpec((None, rows, tile), lambda i: (which, 0, first + i))
    return call(
        functools.partial(product_kernel, blocks),
        token,
        (a, a2, b, b2),
        [whole, whole, b_spec, b_spec],
        [like(width // 2, count)] * 2,
        [pl.BlockSpec((width // 2, tile), lambda i: (0, i))] * 2,
        "side_products",
        6,
        grid=(count // tile,),
    )


def fold_kernel(kept_ref, received_ref, *out_refs):
    height = out_refs[0].shape[0]
    for i, out_ref in enumerate(out_refs):
        part = slice(i * height, (i + 1) * height)
        out = kept_ref[part].astype(f32) + received_ref[part].astype(f32)
        out_ref[...] = out.astype(out_ref.dtype)


def fold(kept, received, last, token):
    rows, width = kept.shape
    whole = pl.BlockSpec(memory_space=pltpu.VMEM)
    outs = [like(rows, width, dtype=f32)] if last else [like(rows // 2, width, dtype=kept.dtype)] * 2
    return call(
        fold_kernel, token, (kept, received), [whole] * 2, outs, [whole] * len(outs), "fold", 1.5,
        room=max(16 * MIB, 4 * MIB + 4 * kept.size * kept.dtype.itemsize),
    )


def hold_kernel(*refs):
    pass


def hold(v, token):
    anywhere = pl.BlockSpec(memory_space=pl.ANY)
    out = like(*v.shape, dtype=v.dtype)
    return call(
        hold_kernel, token, (v,), [anywhere], [out], [anywhere], "hold", 0.1, aliases={0: 0}
    )


def norm_back_kernel(
    mine_ref, theirs_ref, v_ref, gain_ref, base_ref, grad_ref, low_ref, gain_grad_ref
):
    hidden_grad = mine_ref[...].astype(f32) + theirs_ref[...].astype(f32)
    v = v_ref[...].astype(f32)
    scale = rms_scale(v)
    normed = v * scale
    gain_grad = jnp.sum(hidden_grad * normed, axis=0, keepdims=True)

    @pl.when(pl.program_id(0) == 0)
    def _():
        gain_grad_ref[...] = gain_grad

    @pl.when(pl.program_id(0) != 0)
    def _():
        gain_grad_ref[...] += gain_grad

    g = hidden_grad * gain_ref[...]
    out = base_ref[...].astype(f32) + scale * (
        g - normed * jnp.mean(g * normed, axis=-1, keepdims=True)
    )
    grad_ref[...] = out
    low_ref[...] = out.astype(bf16)


def norm_back(mine, theirs, v, gain, base, rows, token):
    total, width = mine.shape
    spec = pl.BlockSpec((rows, width), lambda i: (i, 0))
    row = pl.BlockSpec((1, width), lambda i: (0, 0))
    return call(
        norm_back_kernel,
        token,
        (mine, theirs, v, gain, base),
        [spec, spec, spec, row, spec],
        [like(total, width, dtype=f32), like(total, width), like(1, width, dtype=f32)],
        [spec, spec, row],
        "norm_back",
        6.5,
        grid=(total // rows,),
    )


def local(
    n_dp,
    tokens,
    cotangent,
    active,
    assignment,
    attention_gain,
    query_weight,
    key_weight,
    value_weight,
    out_weight,
    feedforward_gain,
    gate_weight,
    up_weight,
    down_weight,
):
    rows, width = tokens.shape[1:]
    live_seqs = tokens.shape[0] - 1
    total = live_seqs * rows
    block = width // n_dp
    groups = n_dp // 4
    q_cols, k_cols = query_weight.shape[1], key_weight.shape[1]
    hidden_units = gate_weight.shape[1]
    local_kv = k_cols // HD
    group = q_cols // k_cols
    me = lax.axis_index("dp").astype(jnp.int32)

    def flip(v, bits):
        return lax.ppermute(v, "dp", [(i, i ^ bits) for i in range(n_dp)])

    def tensor_flip(v):
        return lax.ppermute(v, "tensor", [(0, 1), (1, 0)])

    def tensor_total(partial_rows):
        mine = lax.optimization_barrier(partial_rows.astype(bf16))
        return mine.astype(f32) + tensor_flip(mine).astype(f32)

    far_bits = [1 << b for b in range(groups.bit_length() - 1)]
    fars = [0]
    for bit in reversed(far_bits):
        fars = fars + [far + bit for far in fars]
    near_places = [far * 4 + pair * 2 for pair in range(2) for far in fars]
    places = near_places + [place + 1 for place in near_places]
    owners = jnp.bitwise_xor(me, jnp.asarray(places, jnp.int32))

    positions = me * rows + jnp.arange(rows, dtype=jnp.int32)
    frequency = jnp.exp(
        -jnp.log(10000.0) * (2.0 * jnp.arange(HD // 2, dtype=f32) / HD)
    )
    angles = positions.astype(f32)[:, None] * frequency[None, :]
    cosine = jnp.concatenate([jnp.cos(angles)] * 2, axis=1)
    sine = jnp.concatenate([-jnp.sin(angles), jnp.sin(angles)], axis=1)
    qpos = jnp.tile(positions, group)[:, None]
    kpos = (owners[:, None] * rows + jnp.arange(rows, dtype=jnp.int32)[None, :]).reshape(1, -1)

    gains = jnp.stack([attention_gain, feedforward_gain], axis=1)
    gains = jnp.pad(gains, ((0, 0), (0, 126)))
    first = lax.all_gather(
        jnp.concatenate([query_weight, key_weight, value_weight, out_weight.T, gains], axis=1),
        "dp", axis=0, tiled=True,
    )
    second = lax.all_gather(
        jnp.concatenate([gate_weight, up_weight, down_weight.T], axis=1), "dp", axis=0, tiled=True
    )
    down_turned = second[:, 2 * hidden_units :]
    qkv_cols = q_cols + 2 * k_cols
    qkv_full = first[:, :qkv_cols]
    out_turned = first[:, qkv_cols : qkv_cols + q_cols]
    gain_attn_row = first[:, qkv_cols + q_cols].astype(f32)[None, :]
    gain_mlp = first[:, qkv_cols + q_cols + 1].astype(f32)[None, :]

    dead_slot = jnp.argmin(active.reshape(-1))
    dead = assignment[dead_slot]
    is_dead = (jnp.arange(live_seqs, dtype=jnp.int32) == dead)[:, None, None]

    def pick(v):
        return jnp.where(is_dead, v[live_seqs:], v[:live_seqs]).reshape(total, width)

    def unpick(live_values, skipped):
        live_values = live_values.reshape(live_seqs, rows, width)
        last = lax.dynamic_slice_in_dim(live_values, jnp.minimum(dead, live_seqs - 1), 1, 0)
        return jnp.concatenate(
            [
                jnp.where(is_dead, skipped[:live_seqs], live_values),
                jnp.where(dead == live_seqs, skipped[live_seqs:], last),
            ],
            axis=0,
        )

    token_low = lax.optimization_barrier(pick(tokens))
    token_rows = token_low.astype(f32)
    down_grad = lax.optimization_barrier(pick(cotangent))

    hidden = (token_rows * rms_scale(token_rows) * gain_attn_row).astype(bf16)
    qkv_raw = dot(hidden, qkv_full, 1, 0)
    queries, kv_own, _ = rope(qkv_raw, cosine, sine, rows, q_cols, k_cols)
    kv_own = kv_own.reshape(1, live_seqs, rows, 2 * k_cols)
    kv_near = kv_own
    for bits in [4 * bit for bit in reversed(far_bits)] + [2]:
        kv_near = jnp.concatenate([kv_near, flip(kv_near, bits)], axis=0)
    kv_other = flip(kv_near, 1)
    mixed_out, log_total = attend(
        queries, kv_near, kv_other, qpos, kpos, rows, local_kv, group
    )
    branch = tensor_total(dot(mixed_out, out_turned, 1, 1))
    middle = token_rows + branch

    hidden_mlp = (middle * rms_scale(middle) * gain_mlp).astype(bf16)
    def side(a):
        keep, send = arrange(a, owners)
        return keep, flip(send, 1)

    token = [None]

    def run(kernel, *args, **kwargs):
        *outs, token[0] = kernel(*args, **kwargs, token=token[0])
        return outs if len(outs) > 1 else outs[0]

    class Total:
        def __init__(self, kept, received, bits):
            self.kept, self.received, self.bits, self.out = kept, received, list(bits), None

        def step(self):
            if self.out is not None:
                return
            if not self.bits:
                self.out = run(fold, self.kept, self.received, True)
                return
            self.kept, sent = run(fold, self.kept, self.received, False)
            self.received = flip(sent, self.bits.pop(0))

        def end(self):
            while self.out is None:
                self.step()
            return self.out

    far_flips = [4 * bit for bit in far_bits]
    far_first = FAR_FIRST if block % 128 == 0 else ()

    def weight_total(name, *args):
        if name in far_first:
            places = [pair * groups + far for far in range(groups) for pair in range(2)]
            spans = [(place * block, (place + 1) * block) for place in places]
            blocks, bits = [spans[:groups], spans[groups:]], [*far_flips, 2]
        else:
            half = groups * block
            blocks, bits = [[(0, half)], [(half, 2 * half)]], [2, *far_flips]
        kept, sent = run(side_products, *args, blocks)
        return Total(kept, flip(sent, bits[0]), bits[1:])

    split_at = -(-hidden_units // 512) * 256
    columns = ((0, split_at), (split_at, hidden_units - split_at))
    down_side, mlp_side, attn_side = side(down_grad), side(hidden_mlp), side(hidden)
    mixed2 = flip(mixed_out, 1)
    arrived = [down_side[1], mlp_side[1], attn_side[1], mixed2]
    (token[0],) = call(hold_kernel, None, (), [], [], [], "hold", 0.1, others=arrived)

    totals, made = {}, {}
    kv_cols = 2 * k_cols
    chunks = {"A": columns[0], "B": columns[1]}

    def send_products(name):
        if name[0] == "d":
            product, product2 = made["product" + name[1]]
            args = (down_side, product[None], product2[None], 0, (0, product.shape[1]))
        elif name[0] in "gu":
            which = "gu".index(name[0])
            args = (mlp_side, made["grads"], made["grads2"], which, chunks[name[1]])
        elif name == "q":
            args = (attn_side, made["qkv_grad"][None], made["qkv_grad2"][None], 0, (0, qkv_cols))
        else:
            args = (made["out_side"], mixed_out[None], mixed2[None], 0, (0, q_cols))
        totals[name] = weight_total(name, *args)

    def feed(name):
        before = made.get("gate_up", ())
        *made["gate_up"], product = run(
            feed_forward, hidden_mlp, second, hidden_units, chunks[name], before
        )
        made["product" + name] = product, flip(product, 1)

    def feed_back():
        made["grads"], made["partial"] = run(
            feed_forward_back, down_grad, *made["gate_up"], second, hidden_units
        )

    def exchange():
        grads, partial = run(hold, made["grads"]), run(hold, made["partial"])
        made.update(grads=grads, grads2=flip(grads, 1), partial=partial, theirs=tensor_flip(partial))

    def middle_back():
        made["middle_grad"], made["branch_grad"], made["gain_mlp"] = run(
            norm_back, made["partial"], made["theirs"], middle, gain_mlp, down_grad, rows
        )

    def mixed_back():
        made["out_side"] = side(made["branch_grad"])
        made["mixed_grad"] = dot(made["branch_grad"], out_turned, 1, 0).astype(bf16)

    def attention_back():
        mixed_grad = made["mixed_grad"]
        made["query_grad"], made["near"], made["other"] = run(
            attend_back, queries, kv_near, kv_other, qpos, kpos, log_total, mixed_grad,
            cosine, sine, rows, local_kv, group, others=[made["out_side"][1]],
        )

    def keys_back():
        other = run(hold, made["other"])
        totals["k"] = Total(
            made["near"].reshape(-1, kv_cols), flip(other.reshape(-1, kv_cols), 1), [2, *far_flips]
        )

    def turn_back():
        dkv = totals["k"].end()
        key_grad, _ = run(
            rope, jnp.concatenate([dkv[:, :k_cols], dkv], axis=1), cosine, -sine, rows, k_cols, k_cols
        )
        qkv_grad = jnp.concatenate(
            [made["query_grad"], key_grad, dkv[:, k_cols:].astype(bf16)], axis=1
        )
        made.update(qkv_grad=qkv_grad, qkv_grad2=flip(qkv_grad, 1))

    def attention_partial():
        made["attn"] = run(times_turned, made["qkv_grad"], first, 0)
        made["attn_theirs"] = tensor_flip(made["attn"])

    def input_back():
        made["input_grad"], _, gain_attn = run(
            norm_back, made["attn"], made["attn_theirs"], token_low, gain_attn_row,
            made["middle_grad"], rows,
        )
        gains = jnp.concatenate([gain_attn, made["gain_mlp"]]).reshape(2, n_dp, block)
        gains = jnp.take(gains, owners, axis=1).transpose(1, 0, 2).reshape(n_dp, 2 * block)
        totals["n"] = Total(gains[: 2 * groups], flip(gains[2 * groups :], 1), [2, *far_flips])

    def down_value():
        product = jnp.concatenate([made["product" + name][0] for name in "AB"], axis=1)
        made["down"] = run(times_turned, product, second, 2)
        made["down_theirs"] = tensor_flip(made["down"])

    actions = {
        "F": feed_back, "H": exchange, "N": middle_back, "M": mixed_back, "A": attention_back, "K": keys_back,
        "R": turn_back, "T": attention_partial, "I": input_back, "V": down_value,
    }
    for entry in ORDER:
        if entry in actions:
            actions[entry]()
        elif entry[0] == "f":
            feed(entry[1])
        elif entry[0] == "P":
            send_products(entry[1:])
        else:
            totals[entry[1:]].step()
    finished = {name: v.end() for name, v in totals.items()}
    down_partial, down_theirs = made["down"], made["down_theirs"]
    input_grad, gains, grad_out, grad_qkv = (
        made["input_grad"], finished["n"], finished["o"], finished["q"],
    )
    grad_down, grad_gate, grad_up = [[finished[m + c] for c in "AB"] for m in "dgu"]
    down_values = down_partial.astype(f32) + down_theirs.astype(f32)
    result = unpick((middle + down_values).astype(bf16), tokens)
    input_grad = unpick(input_grad, cotangent.astype(f32))

    return (
        result,
        input_grad,
        gains[0, :block],
        grad_qkv[:, :q_cols],
        grad_qkv[:, q_cols : q_cols + k_cols],
        grad_qkv[:, q_cols + k_cols :],
        grad_out.T,
        gains[0, block:],
        jnp.concatenate(grad_gate, axis=1),
        jnp.concatenate(grad_up, axis=1),
        jnp.concatenate(grad_down, axis=1).T,
    )


def solution(mesh):
    rows = P(None, "dp", None)
    split = P("dp", "tensor")
    turned = P("tensor", "dp")
    gain = P("dp")
    weights = (gain, split, split, split, turned, gain, split, split, turned)
    return jax.shard_map(
        functools.partial(local, mesh.shape["dp"]),
        mesh=mesh,
        in_specs=(rows, rows, P(), P(), *weights),
        out_specs=(rows, rows, *weights),
        check_vma=False,
    )
```
